256 devices in a mesh: loop: 32 (over z, x_hi, core), slab: 8 (over y, x_lo).
Axes of the slice: x: 4 (x_hi: 2, x_lo: 2; x = x_hi * 2 + x_lo), y: 4, z: 8, core: 2. Of those that a mesh axis runs over, the one named last changes fastest.
Arguments:
- points: bfloat16 [4096, 768], P('loop'), may hold values from -20 to 20
- centroids: bfloat16 [131072, 768], P(('loop', 'slab')), may hold values from -6 to 6
Outputs:
- new_centroids: float32 [131072, 768], P(('loop', 'slab'))
The draws below stay inside these ranges and needn't reach their ends.
All inputs are finite; a program needn't handle non-finite values.
Results may differ from the reference program's by a relative error of at most 0.0007.
Values may be sent and summed in bfloat16 or wider, within the bound.
No kernel may reach another device: no remote copies, remote signals or barrier semaphores. Data moves between devices by JAX's collectives and lax.ppermute only.
A program may use at most 64 MiB of HBM per device.

```python
import math
import jax
import jax.numpy as jnp
from jax import lax

D = 768
POINTS = 4096
CENTS = 131072


def draw_points(key, part):
    key = jax.random.fold_in(key, 11)
    first, second = jax.random.split(key, 2)
    base = jax.random.normal(first, (POINTS, D), jnp.float32)
    scale = jnp.exp(jax.random.uniform(second, (POINTS, 1), jnp.float32, math.log(0.7), math.log(1.4)))
    values = base * scale
    return jnp.clip(values, -20.0, 20.0).astype(jnp.bfloat16)


def block_scale(stream_key, extent, cuts, low, high):
    factor_of, own = 1.0, jax.random.fold_in(stream_key, 6)
    for dim, blocks in cuts:
        steps = jnp.exp(jax.random.uniform(jax.random.fold_in(own, dim), (blocks,), jnp.float32, low / len(cuts), high / len(cuts)))
        factor_of = factor_of * jnp.repeat(steps, extent[dim] // blocks).reshape([-1 if axis == dim else 1 for axis in range(len(extent))])
    return factor_of


def normal_values(own_key, shape, width, reach, cuts=(), held_as=jnp.bfloat16):
    drawn = jax.random.normal(own_key, shape, jnp.float32) * width
    if len(cuts) > 0:
        drawn = block_scale(own_key, shape, cuts, -0.22, 0.18) * drawn
    return jnp.clip(drawn, min=-reach, max=reach).astype(held_as)


def setup_inputs(seed: int = 0) -> dict:
    key_of = jax.random.split(jax.random.key(seed), 3)
    return {
        "points": draw_points(jax.random.fold_in(key_of[2], 71), 0),
        "centroids": normal_values(key_of[1], (CENTS, D), 1.0, 6.0, ((0, 256),)),
    }


SHARP = 20.0
PRIOR = 0.25


def block_logits(xblock, xsq, cblock, csq):
    dots = jnp.dot(xblock, cblock.T, precision=lax.Precision.HIGHEST)
    return -(SHARP / D) * (xsq[:, None] + csq[None, :] - 2.0 * dots)


def reference(points, centroids):
    xf = points.astype(jnp.float32)
    cf = centroids.astype(jnp.float32)
    xsq = jnp.sum(xf * xf, axis=1)
    csq = jnp.sum(cf * cf, axis=1)
    prow = math.gcd(POINTS, 256)
    xs = xf.reshape(POINTS // prow, prow, D)
    xq = xsq.reshape(POINTS // prow, prow)

    def norm_block(pair):
        lg = block_logits(pair[0], pair[1], cf, csq)
        return jax.nn.logsumexp(lg, axis=1)

    lognorm = lax.map(norm_block, (xs, xq)).reshape(POINTS)
    crow = math.gcd(CENTS, 2048)
    cs = cf.reshape(CENTS // crow, crow, D)
    cq = csq.reshape(CENTS // crow, crow)

    def update_block(pair):
        lg = block_logits(xf, xsq, pair[0], pair[1])
        resp = jnp.exp(lg - lognorm[:, None]).astype(jnp.bfloat16).astype(jnp.float32)
        mass = jnp.sum(resp, axis=0)
        sums = jnp.dot(resp.T, xf, precision=lax.Precision.HIGHEST)
        return (sums + PRIOR * pair[0]) / (mass[:, None] + PRIOR)

    return lax.map(update_block, (cs, cq)).reshape(CENTS, D)
```

```python
import functools
import math

import jax
import jax.numpy as jnp
from jax import lax
from jax.experimental import pallas as pl
from jax.experimental.pallas import tpu as pltpu
from jax.sharding import PartitionSpec as P

SHARP = 20.0
PRIOR = 0.25
LOG2E = 1.0 / math.log(2.0)
AXES = ("loop", "slab")
X, Y, Z, C = 4, 4, 8, 2
TILE = 256
LANES = 128
MIB = 1 << 20


def place(device):
    loop, slab = divmod(device, Y * 2)
    z, rest = divmod(loop, 4)
    return (2 * (rest // 2) + slab % 2, slab // 2, z, rest % 2)


def device_at(x, y, z, core):
    return (z * 4 + (x // 2) * 2 + core) * (Y * 2) + y * 2 + x % 2


def send(block, target):
    route = [(d, device_at(*target(*place(d)))) for d in range(X * Y * Z * C)]
    return lax.ppermute(block, AXES, route)


def along_z(block, step):
    return send(block, lambda x, y, z, c: (x, y, (z + step) % Z, c))


def to_sibling(block):
    return send(block, lambda x, y, z, c: (x, y, z, 1 - c))


def combine(parts):
    top = functools.reduce(jnp.maximum, parts)
    return top + jnp.log(sum(jnp.exp2(part - top) for part in parts)) * LOG2E


def prepare_kernel(other_ref, own_ref, both_ref, squares_ref):
    half = own_ref.shape[0]
    for at, ref in enumerate((other_ref, own_ref)):
        block = ref[...]
        both_ref[pl.ds(at * half, half), :] = block
        wide = block.astype(jnp.float32)
        squares_ref[pl.ds(at * half, half), :] = jnp.sum(wide * wide, axis=1, keepdims=True)


def prepare(other, own):
    rows, width = own.shape
    return pl.pallas_call(
        prepare_kernel,
        out_shape=(
            jax.ShapeDtypeStruct((2 * rows, width), own.dtype),
            jax.ShapeDtypeStruct((2 * rows, 1), jnp.float32),
        ),
        compiler_params=pltpu.CompilerParams(vmem_limit_bytes=16 * MIB),
        cost_estimate=pl.CostEstimate(flops=4 * rows * width, bytes_accessed=8 * rows * width, transcendentals=0),
    )(other, own)


def logits_kernel(count, *refs):
    blocks = refs[:count]
    cent_ref, csq_ref, logits_ref, group_ref, norm_ref, xsq_ref, high_ref, total_ref = refs[count:]
    step = pl.program_id(0)
    width = cent_ref.shape[1]
    scale = SHARP / width * LOG2E

    @pl.when(step == 0)
    def _():
        for at, ref in enumerate(blocks):
            rows = ref.shape[0]
            block = ref[...]
            group_ref[pl.ds(at * rows, rows), :] = block
            wide = block.astype(jnp.float32)
            squares = jnp.sum(wide * wide, axis=1, keepdims=True)
            xsq_ref[:, pl.ds(at * rows, rows)] = jnp.broadcast_to(squares, (rows, LANES)).T[:8]
        high_ref[...] = jnp.full_like(high_ref, -jnp.inf)
        total_ref[...] = jnp.zeros_like(total_ref)

    dots = lax.dot_general(
        cent_ref[...], group_ref[...], (((1,), (1,)), ((), ())), preferred_element_type=jnp.float32
    )
    logits = -scale * (xsq_ref[:1, :] + csq_ref[...] - 2.0 * dots)
    logits_ref[...] = logits
    before = high_ref[...]
    top = jnp.maximum(before, jnp.max(logits, axis=0, keepdims=True))
    high_ref[...] = top
    total_ref[...] = total_ref[...] * jnp.exp2(before - top) + jnp.sum(
        jnp.exp2(logits - top), axis=0, keepdims=True
    )

    @pl.when(step == pl.num_programs(0) - 1)
    def _():
        norm_ref[...] = high_ref[...] + jnp.log(total_ref[...]) * LOG2E


def logits_of(blocks, cents, csq):
    rows, width = blocks[0].shape
    points = rows * len(blocks)
    count = cents.shape[0]
    whole = lambda i: (0, 0)
    return pl.pallas_call(
        functools.partial(logits_kernel, len(blocks)),
        grid=(count // TILE,),
        in_specs=[pl.BlockSpec((rows, width), whole)] * len(blocks)
        + [pl.BlockSpec((TILE, width), lambda i: (i, 0)), pl.BlockSpec((TILE, 1), lambda i: (i, 0))],
        out_specs=(
            pl.BlockSpec((TILE, points), lambda i: (i, 0)),
            pl.BlockSpec((points, width), whole),
            pl.BlockSpec((1, points), whole),
        ),
        out_shape=(
            jax.ShapeDtypeStruct((count, points), jnp.float32),
            jax.ShapeDtypeStruct((points, width), blocks[0].dtype),
            jax.ShapeDtypeStruct((1, points), jnp.float32),
        ),
        scratch_shapes=[
            pltpu.VMEM((8, points), jnp.float32),
            pltpu.VMEM((1, points), jnp.float32),
            pltpu.VMEM((1, points), jnp.float32),
        ],
        compiler_params=pltpu.CompilerParams(vmem_limit_bytes=20 * MIB),
        cost_estimate=pl.CostEstimate(
            flops=2 * count * points * width, bytes_accessed=4 * count * points, transcendentals=count * points
        ),
    )(*blocks, cents, csq)


def sums_kernel(groups, *refs):
    logits, blocks = refs[:groups], refs[groups : 2 * groups]
    norm_ref, sums_ref, mass_ref = refs[2 * groups :]
    at = 0
    total, mass = None, None
    for lg_ref, x_ref in zip(logits, blocks):
        points = x_ref.shape[0]
        resp = jnp.exp2(lg_ref[...] - norm_ref[:, pl.ds(at, points)]).astype(jnp.bfloat16)
        part = jnp.dot(resp, x_ref[...], preferred_element_type=jnp.float32)
        wide = resp.astype(jnp.float32)
        weight = sum(wide[:, k : k + LANES] for k in range(0, points, LANES))
        total = part if total is None else total + part
        mass = weight if mass is None else mass + weight
        at += points
    sums_ref[...] = total
    mass_ref[...] = jnp.sum(mass, axis=1, keepdims=True)


def sums_of(logits, blocks, norms, half):
    rows = logits[0].shape[0] // 2
    width = blocks[0].shape[1]
    steps = rows // TILE
    points = norms.shape[1]
    return pl.pallas_call(
        functools.partial(sums_kernel, len(blocks)),
        grid=(steps,),
        in_specs=[pl.BlockSpec((TILE, lg.shape[1]), lambda i: (i + half * steps, 0)) for lg in logits]
        + [pl.BlockSpec(x.shape, lambda i: (0, 0)) for x in blocks]
        + [pl.BlockSpec(norms.shape, lambda i: (0, 0))],
        out_specs=(pl.BlockSpec((TILE, width), lambda i: (i, 0)), pl.BlockSpec((TILE, 1), lambda i: (i, 0))),
        out_shape=(
            jax.ShapeDtypeStruct((rows, width), jnp.float32),
            jax.ShapeDtypeStruct((rows, 1), jnp.float32),
        ),
        compiler_params=pltpu.CompilerParams(vmem_limit_bytes=24 * MIB),
        cost_estimate=pl.CostEstimate(
            flops=2 * rows * points * width, bytes_accessed=4 * rows * points, transcendentals=rows * points
        ),
    )(*logits, *blocks, norms)


def shards(points, centroids):
    loop, slab = lax.axis_index("loop"), lax.axis_index("slab")
    z, x_hi = loop // 4, (loop // 2) % 2
    rows = points.shape[0]

    other_cents = to_sibling(centroids)
    cents, csq = prepare(other_cents, centroids)

    across = send(points, lambda x, y, z, c: (3 - x, y, z, c))
    groups = [[points, across]]
    up, down = [points, across], [points, across]
    for _ in range(3):
        up = [along_z(b, 1) for b in up]
        down = [along_z(b, -1) for b in down]
        groups.append(up + down)
    groups.append([along_z(up[0], 1), along_z(down[1], -1)])

    logits, blocks, norms = zip(*(logits_of(g, cents, csq) for g in groups))

    parts = [n.reshape(-1, rows) for n in norms]
    by_offset = [parts[0]]
    by_offset += [parts[k][2:] for k in (1, 2, 3)] + [parts[4]] + [parts[k][:2] for k in (3, 2, 1)]
    local = jnp.concatenate(by_offset).reshape(Z, 2, rows)
    local = jnp.where(x_hi == 0, local, local[:, ::-1])
    local = lax.dynamic_slice_in_dim(jnp.concatenate([local, local]), Z - z, Z, 0).reshape(Z * 2, rows)

    for kinds in (
        [lambda x, y, z, c, k=k: ((x + k) % X, y, z, c) for k in (1, 2, 3)],
        [lambda x, y, z, c, k=k: (x, (y + k) % Y, z, c) for k in (1, 2, 3)],
        [lambda x, y, z, c, k=k: (x, y, z ^ k, c) for k in (1, 2, 3)],
        [lambda x, y, z, c: (x, y, z ^ 4, c)],
    ):
        local = combine([local] + [send(local, target) for target in kinds])

    total = local.reshape(Z, 2, rows)
    total = lax.dynamic_slice_in_dim(jnp.concatenate([total, total]), z, Z, 0)
    total = jnp.where(x_hi == 0, total, total[:, ::-1])
    ordered = [total[0]]
    for k in (1, 2, 3):
        ordered += [total[Z - k], total[k]]
    ordered.append(total[4])
    lognorm = jnp.concatenate(ordered).reshape(1, -1)

    other_sums, other_mass = sums_of(logits, blocks, lognorm, 0)
    got_sums, got_mass = to_sibling(other_sums), to_sibling(other_mass)
    sums, mass = sums_of(logits, blocks, lognorm, 1)
    sums, mass = sums + got_sums, mass + got_mass
    return (sums + PRIOR * centroids.astype(jnp.float32)) / (mass + PRIOR)


def solution(mesh):
    return jax.shard_map(
        shards,
        mesh=mesh,
        in_specs=(P("loop", None), P(("loop", "slab"), None)),
        out_specs=P(("loop", "slab"), None),
        check_vma=False,
    )
```

```python
import functools
import math

import jax
import jax.numpy as jnp
from jax import lax
from jax.experimental import pallas as pl
from jax.experimental.pallas import tpu as pltpu
from jax.sharding import PartitionSpec as P

SHARP = 20.0
PRIOR = 0.25
LOG2E = 1.0 / math.log(2.0)
AXES = ("loop", "slab")
X, Y, Z, C = 4, 4, 8, 2
TILE = 256
LANES = 128
MIB = 1 << 20


def place(device):
    loop, slab = divmod(device, Y * 2)
    z, rest = divmod(loop, 4)
    return (2 * (rest // 2) + slab % 2, slab // 2, z, rest % 2)


def device_at(x, y, z, core):
    return (z * 4 + (x // 2) * 2 + core) * (Y * 2) + y * 2 + x % 2


def send(block, target):
    route = [(d, device_at(*target(*place(d)))) for d in range(X * Y * Z * C)]
    return lax.ppermute(block, AXES, route)


def along_z(block, step):
    return send(block, lambda x, y, z, c: (x, y, (z + step) % Z, c))


def to_sibling(block):
    return send(block, lambda x, y, z, c: (x, y, z, 1 - c))


def groups_by(key):
    groups = {}
    for d in range(X * Y * Z * C):
        groups.setdefault(key(*place(d)), []).append(d)
    return list(groups.values())


def here(shape, dtype):
    return pltpu.VMEM(shape, dtype)


def pinned(*arrays):
    return [pltpu.with_memory_space_constraint(a, pltpu.VMEM) for a in arrays]


IN_VMEM = pl.BlockSpec(memory_space=pltpu.VMEM)


def combine(parts):
    top = jnp.max(parts, axis=0)
    return top + jnp.log(jnp.sum(jnp.exp2(parts - top), axis=0)) * LOG2E


def prepare_kernel(other_ref, own_ref, both_ref, bias_ref):
    half, width = own_ref.shape
    for at, ref in enumerate((other_ref, own_ref)):
        block = ref[...]
        both_ref[pl.ds(at * half, half), :] = block
        wide = block.astype(jnp.float32)
        squares = jnp.sum(wide * wide, axis=1, keepdims=True)
        bias_ref[pl.ds(at * half, half), :] = jnp.broadcast_to(squares * (SHARP / width * LOG2E), (half, LANES))


def prepare(other, own):
    rows, width = own.shape
    return pl.pallas_call(
        prepare_kernel,
        in_specs=[IN_VMEM, IN_VMEM],
        out_specs=(IN_VMEM, IN_VMEM),
        out_shape=(here((2 * rows, width), own.dtype), here((2 * rows, LANES), jnp.float32)),
        compiler_params=pltpu.CompilerParams(vmem_limit_bytes=8 * MIB),
        cost_estimate=pl.CostEstimate(flops=4 * rows * width, bytes_accessed=8 * rows * width, transcendentals=0),
    )(other, own)


def logits_kernel(count, first, aliased, *refs):
    blocks = refs[:count]
    cent_ref, bias_ref = refs[count : count + 2]
    logits_ref, group_ref, norm_ref, xsq_ref = refs[count + 2 + 3 * aliased :]
    rows, width = blocks[0].shape
    points = rows * count
    scale = SHARP / width * LOG2E
    columns = pl.ds(first, points)
    for at, ref in enumerate(blocks):
        block = ref[...]
        group_ref[pl.ds(first + at * rows, rows), :] = block
        wide = block.astype(jnp.float32)
        squares = jnp.sum(wide * wide, axis=1, keepdims=True) * scale
        xsq_ref[:, pl.ds(at * rows, rows)] = jnp.broadcast_to(squares, (rows, LANES)).T[:8]
    group = group_ref[columns, :]
    xsq = xsq_ref[:1, :]
    tiles = cent_ref.shape[0] // TILE
    high = None
    for t in range(tiles):
        here_rows = pl.ds(t * TILE, TILE)
        dots = lax.dot_general(
            cent_ref[here_rows, :], group, (((1,), (1,)), ((), ())), preferred_element_type=jnp.float32
        )
        bias = jnp.concatenate([bias_ref[here_rows, :]] * (points // LANES), axis=1)
        logits = 2.0 * scale * dots - (bias + xsq)
        logits_ref[here_rows, columns] = logits
        top = jnp.max(logits, axis=0, keepdims=True)
        high = top if high is None else jnp.maximum(high, top)
    total = None
    for t in range(tiles):
        part = jnp.sum(jnp.exp2(logits_ref[pl.ds(t * TILE, TILE), columns] - high), axis=0, keepdims=True)
        total = part if total is None else total + part
    norm_ref[:, columns] = high + jnp.log(total) * LOG2E


def logits_of(blocks, first, points, cents, bias, before):
    rows, width = blocks[0].shape
    count = cents.shape[0]
    more = rows * len(blocks)
    operands = [*blocks, cents, bias, *before]
    return pl.pallas_call(
        functools.partial(logits_kernel, len(blocks), first, len(before) > 0),
        in_specs=[IN_VMEM] * len(operands),
        out_specs=(IN_VMEM,) * 3,
        out_shape=(
            here((count, points), jnp.float32),
            here((points, width), blocks[0].dtype),
            here((1, points), jnp.float32),
        ),
        input_output_aliases={len(blocks) + 2 + k: k for k in range(len(before))},
        scratch_shapes=[pltpu.VMEM((8, more), jnp.float32)],
        compiler_params=pltpu.CompilerParams(vmem_limit_bytes=8 * MIB),
        cost_estimate=pl.CostEstimate(
            flops=2 * count * more * width, bytes_accessed=4 * count * more, transcendentals=count * more
        ),
    )(*pinned(*operands))


def row_of(offset, other):
    loop = lax.axis_index("loop")
    z, x_hi = loop // 4, (loop // 2) % 2
    plane = lax.rem(z + (offset % Z), Z)
    return 2 * plane + (1 - x_hi if other else x_hi)


def arrange_kernel(order, norm_ref, out_ref):
    for k, (offset, other) in enumerate(order):
        out_ref[pl.ds(row_of(offset, other), 1), :] = norm_ref[:, pl.ds(k * LANES, LANES)]


def arrange(order, norms):
    return pl.pallas_call(
        functools.partial(arrange_kernel, order),
        in_specs=[IN_VMEM],
        out_specs=IN_VMEM,
        out_shape=here((len(order), LANES), jnp.float32),
        compiler_params=pltpu.CompilerParams(vmem_limit_bytes=8 * MIB),
    )(*pinned(norms))


def sums_kernel(order, half, logits_ref, group_ref, norms_ref, cent_ref, out_ref, rows_ref, norm_ref):
    rows, width = cent_ref.shape
    points = group_ref.shape[0]
    rows_ref[...] = combine(norms_ref[...])
    for k, (offset, other) in enumerate(order):
        row = rows_ref[pl.ds(row_of(offset, other), 1), :]
        norm_ref[:, pl.ds(k * LANES, LANES)] = jnp.broadcast_to(row, (8, LANES))
    total, mass = None, None
    deep = 512
    for at in range(0, points, deep):
        columns = pl.ds(at, deep)
        logits = logits_ref[pl.ds(half * rows, rows), columns]
        resp = jnp.exp2(logits - norm_ref[:1, columns]).astype(jnp.bfloat16)
        part = jnp.dot(resp, group_ref[columns, :], preferred_element_type=jnp.float32)
        wide = resp.astype(jnp.float32)
        weight = sum(wide[:, k : k + LANES] for k in range(0, deep, LANES))
        total = part if total is None else total + part
        mass = weight if mass is None else mass + weight
    mass = jnp.sum(mass, axis=1, keepdims=True)
    if half == 1:
        total = total + PRIOR * cent_ref[...].astype(jnp.float32)
        mass = mass + PRIOR
    out_ref[:, pl.ds(0, width)] = total
    out_ref[:, pl.ds(width, LANES)] = jnp.broadcast_to(mass, (rows, LANES))


def sums_of(order, half, logits, blocks, norms, cents):
    rows, width = cents.shape
    points = blocks.shape[0]
    return pl.pallas_call(
        functools.partial(sums_kernel, order, half),
        in_specs=[IN_VMEM] * 4,
        out_specs=IN_VMEM,
        out_shape=here((rows, width + LANES), jnp.float32),
        scratch_shapes=[pltpu.VMEM((len(order), LANES), jnp.float32), pltpu.VMEM((8, points), jnp.float32)],
        compiler_params=pltpu.CompilerParams(vmem_limit_bytes=16 * MIB),
        cost_estimate=pl.CostEstimate(
            flops=2 * rows * points * width, bytes_accessed=4 * rows * points, transcendentals=rows * points
        ),
    )(*pinned(logits, blocks, norms, cents))


def finish_kernel(first_ref, second_ref, out_ref):
    rows, width = out_ref.shape
    here_rows = pl.ds(pl.multiple_of(pl.program_id(0) * rows, rows), rows)
    both = first_ref[here_rows, :] + second_ref[here_rows, :]
    weight = 1.0 / both[:, width:]
    out_ref[...] = both[:, :width] * jnp.concatenate([weight] * (width // LANES), axis=1)


def finish(first, second):
    rows, wide = first.shape
    width = wide - LANES
    return pl.pallas_call(
        finish_kernel,
        grid=(4,),
        in_specs=[IN_VMEM] * 2,
        out_specs=pl.BlockSpec((rows // 4, width), lambda i: (i, 0)),
        out_shape=jax.ShapeDtypeStruct((rows, width), jnp.float32),
        compiler_params=pltpu.CompilerParams(vmem_limit_bytes=8 * MIB),
        cost_estimate=pl.CostEstimate(flops=3 * rows * width, bytes_accessed=4 * rows * width, transcendentals=0),
    )(*pinned(first, second))


def after(arrays, *done):
    return lax.optimization_barrier((arrays, done))[0]


def shards(points, centroids):
    rows = points.shape[0]
    everything = rows * Z * 2

    across = send(points, lambda x, y, z, c: (3 - x, y, z, c))
    cents, bias = prepare(to_sibling(centroids), centroids)

    order, state = [], []

    def take(blocks, places):
        nonlocal state
        first = rows * len(order)
        order.extend(places)
        state = logits_of(blocks, first, everything, cents, bias, state)

    own, far = [points, points], [across, across]
    both_ways = lambda pair: [along_z(pair[0], 1), along_z(pair[1], -1)]
    own = both_ways(own)
    far = both_ways(far)
    take([points, across], [(0, 0), (0, 1)])
    for step in (1, 2, 3):
        if step < 3:
            next_own = both_ways(after(own, state[2]))
        else:
            next_own = [along_z(after(own[0], state[2]), 1)]
        take(own, [(-step, 0), (step, 0)])
        if step < 3:
            next_far = both_ways(after(far, state[2]))
        else:
            next_far = [along_z(after(far[1], state[2]), -1)]
        take(far, [(-step, 1), (step, 1)])
        own, far = next_own, next_far
    take([own[0], far[0]], [(4, 0), (4, 1)])
    logits, blocks, norms = state

    local = arrange(order, norms)
    local = combine(
        jnp.stack([local] + [send(local, lambda x, y, z, c, k=k: ((x + k) % X, y, z, c)) for k in (1, 2, 3)])
    )
    everywhere = jnp.broadcast_to(local[None], (Y * Z,) + local.shape)
    parts = lax.all_to_all(everywhere, AXES, 0, 0, axis_index_groups=groups_by(lambda x, y, z, c: (x, c)))

    other_sums = sums_of(order, 0, logits, blocks, parts, centroids)
    got = to_sibling(other_sums)
    own_sums = sums_of(order, 1, logits, blocks, parts, centroids)
    return finish(own_sums, got)


def solution(mesh):
    return jax.shard_map(
        shards,
        mesh=mesh,
        in_specs=(P("loop", None), P(("loop", "slab"), None)),
        out_specs=P(("loop", "slab"), None),
        check_vma=False,
    )
```

```python
import functools
import math

import jax
import jax.numpy as jnp
from jax import lax
from jax.experimental import pallas as pl
from jax.experimental.pallas import tpu as pltpu
from jax.sharding import PartitionSpec as P

SHARP = 20.0
PRIOR = 0.25
LOG2E = 1.0 / math.log(2.0)
AXES = ("loop", "slab")
X, Y, Z, C = 4, 4, 8, 2
TILE = 256
LANES = 128
MIB = 1 << 20


def place(device):
    loop, slab = divmod(device, Y * 2)
    z, rest = divmod(loop, 4)
    return (2 * (rest // 2) + slab % 2, slab // 2, z, rest % 2)


def device_at(x, y, z, core):
    return (z * 4 + (x // 2) * 2 + core) * (Y * 2) + y * 2 + x % 2


def send(block, target):
    route = [(d, device_at(*target(*place(d)))) for d in range(X * Y * Z * C)]
    return lax.ppermute(block, AXES, route)


def along_z(block, step):
    return send(block, lambda x, y, z, c: (x, y, (z + step) % Z, c))


def to_sibling(block):
    return send(block, lambda x, y, z, c: (x, y, z, 1 - c))


def groups_by(key):
    groups = {}
    for d in range(X * Y * Z * C):
        groups.setdefault(key(*place(d)), []).append(d)
    return list(groups.values())


def here(shape, dtype):
    return pltpu.VMEM(shape, dtype)


def pinned(*arrays):
    return [pltpu.with_memory_space_constraint(a, pltpu.VMEM) for a in arrays]


IN_VMEM = pl.BlockSpec(memory_space=pltpu.VMEM)


def combine(parts):
    top = jnp.max(parts, axis=0)
    return top + jnp.log(jnp.sum(jnp.exp2(parts - top), axis=0)) * LOG2E


def prepare_kernel(other_ref, own_ref, both_ref, bias_ref):
    half, width = own_ref.shape
    for at, ref in enumerate((other_ref, own_ref)):
        block = ref[...]
        both_ref[pl.ds(at * half, half), :] = block
        wide = block.astype(jnp.float32)
        squares = jnp.sum(wide * wide, axis=1, keepdims=True)
        bias_ref[pl.ds(at * half, half), :] = jnp.broadcast_to(squares * (SHARP / width * LOG2E), (half, LANES))


def prepare(other, own):
    rows, width = own.shape
    return pl.pallas_call(
        prepare_kernel,
        in_specs=[IN_VMEM, IN_VMEM],
        out_specs=(IN_VMEM, IN_VMEM),
        out_shape=(here((2 * rows, width), own.dtype), here((2 * rows, LANES), jnp.float32)),
        compiler_params=pltpu.CompilerParams(vmem_limit_bytes=8 * MIB),
        cost_estimate=pl.CostEstimate(flops=1, bytes_accessed=1, transcendentals=0),
    )(other, own)


def logits_kernel(count, first, aliased, *refs):
    blocks = refs[:count]
    cent_ref, bias_ref = refs[count : count + 2]
    logits_ref, group_ref, norm_ref, xsq_ref = refs[count + 2 + 3 * aliased :]
    rows, width = blocks[0].shape
    points = rows * count
    scale = SHARP / width * LOG2E
    columns = pl.ds(first, points)
    for at, ref in enumerate(blocks):
        block = ref[...]
        group_ref[pl.ds(first + at * rows, rows), :] = block
        wide = block.astype(jnp.float32)
        squares = jnp.sum(wide * wide, axis=1, keepdims=True) * scale
        xsq_ref[:, pl.ds(at * rows, rows)] = jnp.broadcast_to(squares, (rows, LANES)).T[:8]
    group = group_ref[columns, :]
    xsq = xsq_ref[:1, :]
    tiles = cent_ref.shape[0] // TILE
    high = None
    for t in range(tiles):
        here_rows = pl.ds(t * TILE, TILE)
        dots = lax.dot_general(
            cent_ref[here_rows, :], group, (((1,), (1,)), ((), ())), preferred_element_type=jnp.float32
        )
        bias = jnp.concatenate([bias_ref[here_rows, :]] * (points // LANES), axis=1)
        logits = 2.0 * scale * dots - (bias + xsq)
        logits_ref[here_rows, columns] = logits
        top = jnp.max(logits, axis=0, keepdims=True)
        high = top if high is None else jnp.maximum(high, top)
    total = None
    for t in range(tiles):
        part = jnp.sum(jnp.exp2(logits_ref[pl.ds(t * TILE, TILE), columns] - high), axis=0, keepdims=True)
        total = part if total is None else total + part
    norm_ref[:, columns] = high + jnp.log(total) * LOG2E


def logits_of(blocks, first, points, cents, bias, before):
    rows, width = blocks[0].shape
    count = cents.shape[0]
    more = rows * len(blocks)
    operands = [*blocks, cents, bias, *before]
    return pl.pallas_call(
        functools.partial(logits_kernel, len(blocks), first, len(before) > 0),
        in_specs=[IN_VMEM] * len(operands),
        out_specs=(IN_VMEM,) * 3,
        out_shape=(
            here((count, points), jnp.float32),
            here((points, width), blocks[0].dtype),
            here((1, points), jnp.float32),
        ),
        input_output_aliases={len(blocks) + 2 + k: k for k in range(len(before))},
        scratch_shapes=[pltpu.VMEM((8, more), jnp.float32)],
        compiler_params=pltpu.CompilerParams(vmem_limit_bytes=8 * MIB),
        cost_estimate=pl.CostEstimate(flops=1, bytes_accessed=1, transcendentals=0),
    )(*pinned(*operands))


def row_of(offset, other):
    loop = lax.axis_index("loop")
    z, x_hi = loop // 4, (loop // 2) % 2
    plane = lax.rem(z + (offset % Z), Z)
    return 2 * plane + (1 - x_hi if other else x_hi)


def arrange_kernel(order, norm_ref, out_ref):
    for k, (offset, other) in enumerate(order):
        out_ref[pl.ds(row_of(offset, other), 1), :] = norm_ref[:, pl.ds(k * LANES, LANES)]


def arrange(order, norms):
    return pl.pallas_call(
        functools.partial(arrange_kernel, order),
        in_specs=[IN_VMEM],
        out_specs=IN_VMEM,
        out_shape=here((len(order), LANES), jnp.float32),
        compiler_params=pltpu.CompilerParams(vmem_limit_bytes=8 * MIB),
    )(*pinned(norms))


def sums_kernel(order, half, logits_ref, group_ref, norms_ref, cent_ref, out_ref, rows_ref, norm_ref):
    rows, width = cent_ref.shape
    points = group_ref.shape[0]
    rows_ref[...] = combine(norms_ref[...])
    for k, (offset, other) in enumerate(order):
        row = rows_ref[pl.ds(row_of(offset, other), 1), :]
        norm_ref[:, pl.ds(k * LANES, LANES)] = jnp.broadcast_to(row, (8, LANES))
    total, mass = None, None
    deep = 512
    for at in range(0, points, deep):
        columns = pl.ds(at, deep)
        logits = logits_ref[pl.ds(half * rows, rows), columns]
        resp = jnp.exp2(logits - norm_ref[:1, columns]).astype(jnp.bfloat16)
        part = jnp.dot(resp, group_ref[columns, :], preferred_element_type=jnp.float32)
        wide = resp.astype(jnp.float32)
        weight = sum(wide[:, k : k + LANES] for k in range(0, deep, LANES))
        total = part if total is None else total + part
        mass = weight if mass is None else mass + weight
    mass = jnp.sum(mass, axis=1, keepdims=True)
    if half == 1:
        total = total + PRIOR * cent_ref[...].astype(jnp.float32)
        mass = mass + PRIOR
    out_ref[:, pl.ds(0, width)] = total
    out_ref[:, pl.ds(width, LANES)] = jnp.broadcast_to(mass, (rows, LANES))


def sums_of(order, half, logits, blocks, norms, cents):
    rows, width = cents.shape
    points = blocks.shape[0]
    return pl.pallas_call(
        functools.partial(sums_kernel, order, half),
        in_specs=[IN_VMEM] * 4,
        out_specs=IN_VMEM,
        out_shape=here((rows, width + LANES), jnp.float32),
        scratch_shapes=[pltpu.VMEM((len(order), LANES), jnp.float32), pltpu.VMEM((8, points), jnp.float32)],
        compiler_params=pltpu.CompilerParams(vmem_limit_bytes=16 * MIB),
        cost_estimate=pl.CostEstimate(
            flops=2 * rows * points * width, bytes_accessed=4 * rows * points, transcendentals=rows * points
        ),
    )(*pinned(logits, blocks, norms, cents))


def finish_kernel(first_ref, second_ref, out_ref):
    rows, width = out_ref.shape
    here_rows = pl.ds(pl.multiple_of(pl.program_id(0) * rows, rows), rows)
    both = first_ref[here_rows, :] + second_ref[here_rows, :]
    weight = 1.0 / both[:, width:]
    out_ref[...] = both[:, :width] * jnp.concatenate([weight] * (width // LANES), axis=1)


def finish(first, second):
    rows, wide = first.shape
    width = wide - LANES
    return pl.pallas_call(
        finish_kernel,
        grid=(4,),
        in_specs=[IN_VMEM] * 2,
        out_specs=pl.BlockSpec((rows // 4, width), lambda i: (i, 0)),
        out_shape=jax.ShapeDtypeStruct((rows, width), jnp.float32),
        compiler_params=pltpu.CompilerParams(vmem_limit_bytes=8 * MIB),
        cost_estimate=pl.CostEstimate(flops=3 * rows * width, bytes_accessed=4 * rows * width, transcendentals=0),
    )(*pinned(first, second))


def after(arrays, *done):
    return lax.optimization_barrier((arrays, done))[0]


def shards(points, centroids):
    rows = points.shape[0]
    everything = rows * Z * 2

    across = send(points, lambda x, y, z, c: (3 - x, y, z, c))
    cents, bias = prepare(to_sibling(centroids), centroids)

    order, state = [], []

    def take(blocks, places):
        nonlocal state
        first = rows * len(order)
        order.extend(places)
        state = logits_of(blocks, first, everything, cents, bias, state)

    own, far = [points, points], [across, across]
    both_ways = lambda pair: [along_z(pair[0], 1), along_z(pair[1], -1)]
    own = both_ways(own)
    far = both_ways(far)
    pending = [([points, across], [(0, 0), (0, 1)])]
    for step in (1, 2, 3):
        seen = [] if step == 1 else state[2]
        if step < 3:
            next_own = both_ways(after(own, seen))
        else:
            next_own = [along_z(after(own[0], seen), 1)]
        take(*pending.pop(0))
        seen = state[2]
        if step < 3:
            next_far = both_ways(after(far, seen))
        else:
            next_far = [along_z(after(far[1], seen), -1)]
        if step > 1:
            take(*pending.pop(0))
        pending.append((own, [(-step, 0), (step, 0)]))
        pending.append((far, [(-step, 1), (step, 1)]))
        own, far = next_own, next_far
    pending.append(([own[0], far[0]], [(4, 0), (4, 1)]))
    for blocks, places in pending:
        take(blocks, places)
    logits, blocks, norms = state

    local = arrange(order, norms)
    local = combine(
        jnp.stack([local] + [send(local, lambda x, y, z, c, k=k: ((x + k) % X, y, z, c)) for k in (1, 2, 3)])
    )
    everywhere = jnp.broadcast_to(local[None], (Y * Z,) + local.shape)
    parts = lax.all_to_all(everywhere, AXES, 0, 0, axis_index_groups=groups_by(lambda x, y, z, c: (x, c)))

    other_sums = sums_of(order, 0, logits, blocks, parts, centroids)
    got = to_sibling(other_sums)
    own_sums = sums_of(order, 1, logits, blocks, parts, centroids)
    return finish(own_sums, got)


def solution(mesh):
    return jax.shard_map(
        shards,
        mesh=mesh,
        in_specs=(P("loop", None), P(("loop", "slab"), None)),
        out_specs=P(("loop", "slab"), None),
        check_vma=False,
    )
```

```python
import functools
import math

import jax
import jax.numpy as jnp
from jax import lax
from jax.experimental import pallas as pl
from jax.experimental.pallas import tpu as pltpu
from jax.sharding import PartitionSpec as P

SHARP = 20.0
PRIOR = 0.25
LOG2E = 1.0 / math.log(2.0)
AXES = ("loop", "slab")
X, Y, Z, C = 4, 4, 8, 2
TILE = 256
LANES = 128
MIB = 1 << 20


def place(device):
    loop, slab = divmod(device, Y * 2)
    z, rest = divmod(loop, 4)
    return (2 * (rest // 2) + slab % 2, slab // 2, z, rest % 2)


def device_at(x, y, z, core):
    return (z * 4 + (x // 2) * 2 + core) * (Y * 2) + y * 2 + x % 2


def send(block, target):
    route = [(d, device_at(*target(*place(d)))) for d in range(X * Y * Z * C)]
    return lax.ppermute(block, AXES, route)


def along_z(block, step):
    return send(block, lambda x, y, z, c: (x, y, (z + step) % Z, c))


def to_sibling(block):
    return send(block, lambda x, y, z, c: (x, y, z, 1 - c))


def groups_by(key):
    groups = {}
    for d in range(X * Y * Z * C):
        groups.setdefault(key(*place(d)), []).append(d)
    return list(groups.values())


def here(shape, dtype):
    return pltpu.VMEM(shape, dtype)


def pinned(*arrays):
    return [pltpu.with_memory_space_constraint(a, pltpu.VMEM) for a in arrays]


IN_VMEM = pl.BlockSpec(memory_space=pltpu.VMEM)


def combine(parts):
    top = jnp.max(parts, axis=0)
    return top + jnp.log(jnp.sum(jnp.exp2(parts - top), axis=0)) * LOG2E


def prepare_kernel(other_ref, own_ref, both_ref, bias_ref):
    half, width = own_ref.shape
    for at, ref in enumerate((other_ref, own_ref)):
        block = ref[...]
        both_ref[pl.ds(at * half, half), :] = block
        wide = block.astype(jnp.float32)
        squares = jnp.sum(wide * wide, axis=1, keepdims=True)
        bias_ref[pl.ds(at * half, half), :] = jnp.broadcast_to(squares * (SHARP / width * LOG2E), (half, LANES))


def prepare(other, own):
    rows, width = own.shape
    return pl.pallas_call(
        prepare_kernel,
        in_specs=[IN_VMEM, IN_VMEM],
        out_specs=(IN_VMEM, IN_VMEM),
        out_shape=(here((2 * rows, width), own.dtype), here((2 * rows, LANES), jnp.float32)),
        compiler_params=pltpu.CompilerParams(vmem_limit_bytes=8 * MIB),
        cost_estimate=pl.CostEstimate(flops=1, bytes_accessed=1, transcendentals=0),
    )(other, own)


def logits_kernel(count, first, aliased, *refs):
    blocks = refs[:count]
    cent_ref, bias_ref = refs[count : count + 2]
    logits_ref, group_ref, norm_ref, xsq_ref = refs[count + 2 + 3 * aliased :]
    rows, width = blocks[0].shape
    points = rows * count
    scale = SHARP / width * LOG2E
    columns = pl.ds(first, points)
    for at, ref in enumerate(blocks):
        block = ref[...]
        group_ref[pl.ds(first + at * rows, rows), :] = block
        wide = block.astype(jnp.float32)
        squares = jnp.sum(wide * wide, axis=1, keepdims=True) * scale
        xsq_ref[:, pl.ds(at * rows, rows)] = jnp.broadcast_to(squares, (rows, LANES)).T[:8]
    group = group_ref[columns, :]
    xsq = xsq_ref[:1, :]
    tiles = cent_ref.shape[0] // TILE
    high = None
    for t in range(tiles):
        here_rows = pl.ds(t * TILE, TILE)
        dots = lax.dot_general(
            cent_ref[here_rows, :], group, (((1,), (1,)), ((), ())), preferred_element_type=jnp.float32
        )
        bias = jnp.concatenate([bias_ref[here_rows, :]] * (points // LANES), axis=1)
        logits = 2.0 * scale * dots - (bias + xsq)
        logits_ref[here_rows, columns] = logits
        top = jnp.max(logits, axis=0, keepdims=True)
        high = top if high is None else jnp.maximum(high, top)
    total = None
    for t in range(tiles):
        part = jnp.sum(jnp.exp2(logits_ref[pl.ds(t * TILE, TILE), columns] - high), axis=0, keepdims=True)
        total = part if total is None else total + part
    norm_ref[:, columns] = high + jnp.log(total) * LOG2E


def logits_of(blocks, first, points, cents, bias, before):
    rows, width = blocks[0].shape
    count = cents.shape[0]
    more = rows * len(blocks)
    operands = [*blocks, cents, bias, *before]
    return pl.pallas_call(
        functools.partial(logits_kernel, len(blocks), first, len(before) > 0),
        in_specs=[IN_VMEM] * len(operands),
        out_specs=(IN_VMEM,) * 3,
        out_shape=(
            here((count, points), jnp.float32),
            here((points, width), blocks[0].dtype),
            here((1, points), jnp.float32),
        ),
        input_output_aliases={len(blocks) + 2 + k: k for k in range(len(before))},
        scratch_shapes=[pltpu.VMEM((8, more), jnp.float32)],
        compiler_params=pltpu.CompilerParams(vmem_limit_bytes=8 * MIB),
        cost_estimate=pl.CostEstimate(flops=1, bytes_accessed=1, transcendentals=0),
    )(*pinned(*operands))


def row_of(offset, other):
    loop = lax.axis_index("loop")
    z, x_hi = loop // 4, (loop // 2) % 2
    plane = lax.rem(z + (offset % Z), Z)
    return 2 * plane + (1 - x_hi if other else x_hi)


def arrange_kernel(order, norm_ref, out_ref):
    for k, (offset, other) in enumerate(order):
        out_ref[pl.ds(row_of(offset, other), 1), :] = norm_ref[:, pl.ds(k * LANES, LANES)]


def arrange(order, norms):
    return pl.pallas_call(
        functools.partial(arrange_kernel, order),
        in_specs=[IN_VMEM],
        out_specs=IN_VMEM,
        out_shape=here((len(order), LANES), jnp.float32),
        compiler_params=pltpu.CompilerParams(vmem_limit_bytes=8 * MIB),
    )(*pinned(norms))


def spread_kernel(order, parts_ref, norm_ref, rows_ref):
    rows_ref[...] = combine(parts_ref[...])
    for k, (offset, other) in enumerate(order):
        row = rows_ref[pl.ds(row_of(offset, other), 1), :]
        norm_ref[:, pl.ds(k * LANES, LANES)] = jnp.broadcast_to(row, (8, LANES))


def add_up(logits_ref, start, group_ref, norm_ref, cent_ref, out_ref):
    rows, width = out_ref.shape[0], group_ref.shape[1]
    points = group_ref.shape[0]
    total, mass = None, None
    deep = 512
    for at in range(0, points, deep):
        columns = pl.ds(at, deep)
        logits = logits_ref[pl.ds(start, rows), columns]
        resp = jnp.exp2(logits - norm_ref[:1, columns]).astype(jnp.bfloat16)
        part = jnp.dot(resp, group_ref[columns, :], preferred_element_type=jnp.float32)
        wide = resp.astype(jnp.float32)
        weight = sum(wide[:, k : k + LANES] for k in range(0, deep, LANES))
        total = part if total is None else total + part
        mass = weight if mass is None else mass + weight
    mass = jnp.sum(mass, axis=1, keepdims=True)
    if cent_ref is not None:
        total = total + PRIOR * cent_ref[...].astype(jnp.float32)
        mass = mass + PRIOR
    out_ref[:, pl.ds(0, width)] = total
    out_ref[:, pl.ds(width, LANES)] = jnp.broadcast_to(mass, (rows, LANES))


def first_sums_kernel(order, start, logits_ref, group_ref, parts_ref, out_ref, norm_ref, rows_ref):
    spread_kernel(order, parts_ref, norm_ref, rows_ref)
    add_up(logits_ref, start, group_ref, norm_ref, None, out_ref)


def more_sums_kernel(start, logits_ref, group_ref, norm_ref, out_ref):
    add_up(logits_ref, start, group_ref, norm_ref, None, out_ref)


def own_sums_kernel(start, logits_ref, group_ref, norm_ref, cent_ref, out_ref):
    add_up(logits_ref, start, group_ref, norm_ref, cent_ref, out_ref)


def sums_call(kernel, operands, rows, points, width, spread=None):
    out = here((rows, width + LANES), jnp.float32)
    return pl.pallas_call(
        kernel,
        in_specs=[IN_VMEM] * len(operands),
        out_specs=(IN_VMEM, IN_VMEM) if spread else IN_VMEM,
        out_shape=(out, here((8, points), jnp.float32)) if spread else out,
        scratch_shapes=[pltpu.VMEM((spread, LANES), jnp.float32)] if spread else [],
        compiler_params=pltpu.CompilerParams(vmem_limit_bytes=16 * MIB),
        cost_estimate=pl.CostEstimate(flops=1, bytes_accessed=1, transcendentals=0),
    )(*pinned(*operands))


def finish_kernel(own_ref, *refs):
    out_ref = refs[-1]
    rows, width = out_ref.shape
    for k, ref in enumerate(refs[:-1]):

        @pl.when(pl.program_id(0) == k)
        def _():
            both = own_ref[pl.ds(k * rows, rows), :] + ref[...]
            weight = 1.0 / both[:, width:]
            out_ref[...] = both[:, :width] * jnp.concatenate([weight] * (width // LANES), axis=1)


def finish(own, others):
    rows, wide = own.shape
    width = wide - LANES
    steps = len(others)
    return pl.pallas_call(
        finish_kernel,
        grid=(steps,),
        in_specs=[IN_VMEM] * (1 + steps),
        out_specs=pl.BlockSpec((rows // steps, width), lambda i: (i, 0)),
        out_shape=jax.ShapeDtypeStruct((rows, width), jnp.float32),
        compiler_params=pltpu.CompilerParams(vmem_limit_bytes=8 * MIB),
        cost_estimate=pl.CostEstimate(flops=3 * rows * width, bytes_accessed=4 * rows * width, transcendentals=0),
    )(*pinned(own, *others))


def after(arrays, *done):
    return lax.optimization_barrier((arrays, done))[0]


def shards(points, centroids):
    rows = points.shape[0]
    everything = rows * Z * 2

    across = send(points, lambda x, y, z, c: (3 - x, y, z, c))
    cents, bias = prepare(to_sibling(centroids), centroids)

    order, state = [], []

    def take(blocks, places):
        nonlocal state
        first = rows * len(order)
        order.extend(places)
        state = logits_of(blocks, first, everything, cents, bias, state)

    own, far = [points, points], [across, across]
    both_ways = lambda pair: [along_z(pair[0], 1), along_z(pair[1], -1)]
    own = both_ways(own)
    far = both_ways(far)
    pending = [([points, across], [(0, 0), (0, 1)])]
    for step in (1, 2, 3):
        seen = [] if step == 1 else state[2]
        if step < 3:
            next_own = both_ways(after(own, seen))
        else:
            next_own = [along_z(after(own[0], seen), 1)]
        take(*pending.pop(0))
        seen = state[2]
        if step < 3:
            next_far = both_ways(after(far, seen))
        else:
            next_far = [along_z(after(far[1], seen), -1)]
        if step > 1:
            take(*pending.pop(0))
        pending.append((own, [(-step, 0), (step, 0)]))
        pending.append((far, [(-step, 1), (step, 1)]))
        own, far = next_own, next_far
    pending.append(([own[0], far[0]], [(4, 0), (4, 1)]))
    for blocks, places in pending:
        take(blocks, places)
    logits, blocks, norms = state

    local = arrange(order, norms)
    local = combine(
        jnp.stack([local] + [send(local, lambda x, y, z, c, k=k: ((x + k) % X, y, z, c)) for k in (1, 2, 3)])
    )
    everywhere = jnp.broadcast_to(local[None], (Y * Z,) + local.shape)
    parts = lax.all_to_all(everywhere, AXES, 0, 0, axis_index_groups=groups_by(lambda x, y, z, c: (x, c)))

    count, width = centroids.shape
    piece = count // 2
    shape = (everything, width)
    one, norm = sums_call(
        functools.partial(first_sums_kernel, tuple(order), 0), (logits, blocks, parts), piece, *shape, len(order)
    )
    got_one = to_sibling(one)
    two = sums_call(functools.partial(more_sums_kernel, piece), (logits, blocks, norm), piece, *shape)
    got_two = to_sibling(two)
    norm = after(norm, two)
    own_sums = sums_call(
        functools.partial(own_sums_kernel, count), (logits, blocks, norm, centroids), count, *shape
    )
    return finish(own_sums, (got_one, got_two))


def solution(mesh):
    return jax.shard_map(
        shards,
        mesh=mesh,
        in_specs=(P("loop", None), P(("loop", "slab"), None)),
        out_specs=P(("loop", "slab"), None),
        check_vma=False,
    )
```

```python
import functools
import math

import jax
import jax.numpy as jnp
from jax import lax
from jax.experimental import pallas as pl
from jax.experimental.pallas import tpu as pltpu
from jax.sharding import PartitionSpec as P

SHARP = 20.0
PRIOR = 0.25
LOG2E = 1.0 / math.log(2.0)
AXES = ("loop", "slab")
X, Y, Z, C = 4, 4, 8, 2
TILE = 256
LANES = 128
MIB = 1 << 20


def place(device):
    loop, slab = divmod(device, Y * 2)
    z, rest = divmod(loop, 4)
    return (2 * (rest // 2) + slab % 2, slab // 2, z, rest % 2)


def device_at(x, y, z, core):
    return (z * 4 + (x // 2) * 2 + core) * (Y * 2) + y * 2 + x % 2


def send(block, target):
    route = [(d, device_at(*target(*place(d)))) for d in range(X * Y * Z * C)]
    return lax.ppermute(block, AXES, route)


def along_z(block, step):
    return send(block, lambda x, y, z, c: (x, y, (z + step) % Z, c))


def to_sibling(block):
    return send(block, lambda x, y, z, c: (x, y, z, 1 - c))


def groups_by(key):
    groups = {}
    for d in range(X * Y * Z * C):
        groups.setdefault(key(*place(d)), []).append(d)
    return list(groups.values())


def here(shape, dtype):
    return pltpu.VMEM(shape, dtype)


def pinned(*arrays):
    return [pltpu.with_memory_space_constraint(a, pltpu.VMEM) for a in arrays]


IN_VMEM = pl.BlockSpec(memory_space=pltpu.VMEM)


def combine(parts):
    top = jnp.max(parts, axis=0)
    return top + jnp.log(jnp.sum(jnp.exp2(parts - top), axis=0)) * LOG2E


def prepare_kernel(other_ref, own_ref, both_ref, bias_ref):
    half, width = own_ref.shape
    for at, ref in enumerate((other_ref, own_ref)):
        block = ref[...]
        both_ref[pl.ds(at * half, half), :] = block
        wide = block.astype(jnp.float32)
        squares = jnp.sum(wide * wide, axis=1, keepdims=True)
        bias_ref[pl.ds(at * half, half), :] = jnp.broadcast_to(squares * (SHARP / width * LOG2E), (half, LANES))


def prepare(other, own):
    rows, width = own.shape
    return pl.pallas_call(
        prepare_kernel,
        in_specs=[IN_VMEM, IN_VMEM],
        out_specs=(IN_VMEM, IN_VMEM),
        out_shape=(here((2 * rows, width), own.dtype), here((2 * rows, LANES), jnp.float32)),
        compiler_params=pltpu.CompilerParams(vmem_limit_bytes=8 * MIB),
        cost_estimate=pl.CostEstimate(flops=1, bytes_accessed=1, transcendentals=0),
    )(other, own)


def logits_kernel(count, first, aliased, *refs):
    blocks = refs[:count]
    cent_ref, bias_ref = refs[count : count + 2]
    logits_ref, group_ref, norm_ref, xsq_ref = refs[count + 2 + 3 * aliased :]
    rows, width = blocks[0].shape
    points = rows * count
    scale = SHARP / width * LOG2E
    columns = pl.ds(first, points)
    for at, ref in enumerate(blocks):
        block = ref[...]
        group_ref[pl.ds(first + at * rows, rows), :] = block
        wide = block.astype(jnp.float32)
        squares = jnp.sum(wide * wide, axis=1, keepdims=True) * scale
        xsq_ref[:, pl.ds(at * rows, rows)] = jnp.broadcast_to(squares, (rows, LANES)).T[:8]
    group = group_ref[columns, :]
    xsq = xsq_ref[:1, :]
    tiles = cent_ref.shape[0] // TILE
    high = None
    for t in range(tiles):
        here_rows = pl.ds(t * TILE, TILE)
        dots = lax.dot_general(
            cent_ref[here_rows, :], group, (((1,), (1,)), ((), ())), preferred_element_type=jnp.float32
        )
        bias = jnp.concatenate([bias_ref[here_rows, :]] * (points // LANES), axis=1)
        logits = 2.0 * scale * dots - (bias + xsq)
        logits_ref[here_rows, columns] = logits
        top = jnp.max(logits, axis=0, keepdims=True)
        high = top if high is None else jnp.maximum(high, top)
    total = None
    for t in range(tiles):
        part = jnp.sum(jnp.exp2(logits_ref[pl.ds(t * TILE, TILE), columns] - high), axis=0, keepdims=True)
        total = part if total is None else total + part
    norm_ref[:, columns] = high + jnp.log(total) * LOG2E


def logits_of(blocks, first, points, cents, bias, before):
    rows, width = blocks[0].shape
    count = cents.shape[0]
    more = rows * len(blocks)
    operands = [*blocks, cents, bias, *before]
    return pl.pallas_call(
        functools.partial(logits_kernel, len(blocks), first, len(before) > 0),
        in_specs=[IN_VMEM] * len(operands),
        out_specs=(IN_VMEM,) * 3,
        out_shape=(
            here((count, points), jnp.float32),
            here((points, width), blocks[0].dtype),
            here((1, points), jnp.float32),
        ),
        input_output_aliases={len(blocks) + 2 + k: k for k in range(len(before))},
        scratch_shapes=[pltpu.VMEM((8, more), jnp.float32)],
        compiler_params=pltpu.CompilerParams(vmem_limit_bytes=8 * MIB),
        cost_estimate=pl.CostEstimate(flops=1, bytes_accessed=1, transcendentals=0),
    )(*pinned(*operands))


def row_of(offset, other):
    loop = lax.axis_index("loop")
    z, x_hi = loop // 4, (loop // 2) % 2
    plane = lax.rem(z + (offset % Z), Z)
    return 2 * plane + (1 - x_hi if other else x_hi)


def arrange_kernel(order, norm_ref, out_ref):
    for k, (offset, other) in enumerate(order):
        out_ref[pl.ds(row_of(offset, other), 1), :] = norm_ref[:, pl.ds(k * LANES, LANES)]


def arrange(order, norms):
    return pl.pallas_call(
        functools.partial(arrange_kernel, order),
        in_specs=[IN_VMEM],
        out_specs=IN_VMEM,
        out_shape=here((len(order), LANES), jnp.float32),
        compiler_params=pltpu.CompilerParams(vmem_limit_bytes=8 * MIB),
    )(*pinned(norms))


def spread_kernel(order, parts_ref, norm_ref, rows_ref):
    rows_ref[...] = combine(parts_ref[...])
    for k, (offset, other) in enumerate(order):
        row = rows_ref[pl.ds(row_of(offset, other), 1), :]
        norm_ref[:, pl.ds(k * LANES, LANES)] = jnp.broadcast_to(row, (8, LANES))


def add_up(logits_ref, start, group_ref, norm_ref, cent_ref, out_ref):
    rows, width = out_ref.shape[0], group_ref.shape[1]
    points = group_ref.shape[0]
    total, mass = None, None
    deep = 512
    for at in range(0, points, deep):
        columns = pl.ds(at, deep)
        logits = logits_ref[pl.ds(start, rows), columns]
        resp = jnp.exp2(logits - norm_ref[:1, columns]).astype(jnp.bfloat16)
        part = jnp.dot(resp, group_ref[columns, :], preferred_element_type=jnp.float32)
        wide = resp.astype(jnp.float32)
        weight = sum(wide[:, k : k + LANES] for k in range(0, deep, LANES))
        total = part if total is None else total + part
        mass = weight if mass is None else mass + weight
    mass = jnp.sum(mass, axis=1, keepdims=True)
    if cent_ref is not None:
        total = total + PRIOR * cent_ref[...].astype(jnp.float32)
        mass = mass + PRIOR
    out_ref[:, pl.ds(0, width)] = total
    out_ref[:, pl.ds(width, LANES)] = jnp.broadcast_to(mass, (rows, LANES))


def first_sums_kernel(order, start, logits_ref, group_ref, parts_ref, out_ref, norm_ref, rows_ref):
    spread_kernel(order, parts_ref, norm_ref, rows_ref)
    add_up(logits_ref, start, group_ref, norm_ref, None, out_ref)


def more_sums_kernel(start, logits_ref, group_ref, norm_ref, out_ref):
    add_up(logits_ref, start, group_ref, norm_ref, None, out_ref)


def own_sums_kernel(start, logits_ref, group_ref, norm_ref, cent_ref, out_ref):
    add_up(logits_ref, start, group_ref, norm_ref, cent_ref, out_ref)


def sums_call(kernel, operands, rows, points, width, spread=None):
    out = here((rows, width + LANES), jnp.float32)
    return pl.pallas_call(
        kernel,
        in_specs=[IN_VMEM] * len(operands),
        out_specs=(IN_VMEM, IN_VMEM) if spread else IN_VMEM,
        out_shape=(out, here((8, points), jnp.float32)) if spread else out,
        scratch_shapes=[pltpu.VMEM((spread, LANES), jnp.float32)] if spread else [],
        compiler_params=pltpu.CompilerParams(vmem_limit_bytes=16 * MIB),
        cost_estimate=pl.CostEstimate(flops=1, bytes_accessed=1, transcendentals=0),
    )(*pinned(*operands))


def finish_kernel(own_ref, *refs):
    out_ref = refs[-1]
    rows, width = out_ref.shape
    first = 0
    for ref in refs[:-1]:
        last = first + ref.shape[0]
        for step in range(own_ref.shape[0] // rows):
            start, stop = max(first, step * rows), min(last, (step + 1) * rows)
            if start >= stop:
                continue

            @pl.when(pl.program_id(0) == step)
            def _():
                both = own_ref[pl.ds(start, stop - start), :] + ref[pl.ds(start - first, stop - start), :]
                weight = 1.0 / both[:, width:]
                out_ref[pl.ds(start - step * rows, stop - start), :] = both[:, :width] * jnp.concatenate(
                    [weight] * (width // LANES), axis=1
                )

        first = last


def finish(own, others):
    rows, wide = own.shape
    width = wide - LANES
    steps = 2
    return pl.pallas_call(
        finish_kernel,
        grid=(steps,),
        in_specs=[IN_VMEM] * (1 + len(others)),
        out_specs=pl.BlockSpec((rows // steps, width), lambda i: (i, 0)),
        out_shape=jax.ShapeDtypeStruct((rows, width), jnp.float32),
        compiler_params=pltpu.CompilerParams(vmem_limit_bytes=8 * MIB),
        cost_estimate=pl.CostEstimate(flops=3 * rows * width, bytes_accessed=4 * rows * width, transcendentals=0),
    )(*pinned(own, *others))


def after(arrays, *done):
    return lax.optimization_barrier((arrays, done))[0]


def shards(points, centroids):
    rows = points.shape[0]
    everything = rows * Z * 2

    across = send(points, lambda x, y, z, c: (3 - x, y, z, c))
    cents, bias = prepare(to_sibling(centroids), centroids)

    order, state = [], []

    def take(blocks, places):
        nonlocal state
        first = rows * len(order)
        order.extend(places)
        state = logits_of(blocks, first, everything, cents, bias, state)

    own, far = [points, points], [across, across]
    both_ways = lambda pair: [along_z(pair[0], 1), along_z(pair[1], -1)]
    own = both_ways(own)
    far = both_ways(far)
    pending = [([points, across], [(0, 0), (0, 1)])]
    for step in (1, 2, 3):
        seen = [] if step == 1 else state[2]
        if step < 3:
            next_own = both_ways(after(own, seen))
        else:
            next_own = [along_z(after(own[0], seen), 1)]
        take(*pending.pop(0))
        seen = state[2]
        if step < 3:
            next_far = both_ways(after(far, seen))
        else:
            next_far = [along_z(after(far[1], seen), -1)]
        if step > 1:
            take(*pending.pop(0))
        pending.append((own, [(-step, 0), (step, 0)]))
        pending.append((far, [(-step, 1), (step, 1)]))
        own, far = next_own, next_far
    pending.append(([own[0], far[0]], [(4, 0), (4, 1)]))
    for blocks, places in pending:
        take(blocks, places)
    logits, blocks, norms = state

    local = arrange(order, norms)
    local = combine(
        jnp.stack([local] + [send(local, lambda x, y, z, c, k=k: ((x + k) % X, y, z, c)) for k in (2, 1, 3)])
    )
    everywhere = jnp.broadcast_to(local[None], (Y * Z,) + local.shape)
    parts = lax.all_to_all(everywhere, AXES, 0, 0, axis_index_groups=groups_by(lambda x, y, z, c: (x, c)))

    count, width = centroids.shape
    piece = count * 5 // 8
    shape = (everything, width)
    one, norm = sums_call(
        functools.partial(first_sums_kernel, tuple(order), 0), (logits, blocks, parts), piece, *shape, len(order)
    )
    got_one = to_sibling(one)
    two = sums_call(functools.partial(more_sums_kernel, piece), (logits, blocks, norm), count - piece, *shape)
    got_two = to_sibling(two)
    norm = after(norm, two)
    own_sums = sums_call(
        functools.partial(own_sums_kernel, count), (logits, blocks, norm, centroids), count, *shape
    )
    return finish(own_sums, (got_one, got_two))


def solution(mesh):
    return jax.shard_map(
        shards,
        mesh=mesh,
        in_specs=(P("loop", None), P(("loop", "slab"), None)),
        out_specs=P(("loop", "slab"), None),
        check_vma=False,
    )
```

```python
import functools
import math

import jax
import jax.numpy as jnp
from jax import lax
from jax.experimental import pallas as pl
from jax.experimental.pallas import tpu as pltpu
from jax.sharding import PartitionSpec as P

SHARP = 20.0
PRIOR = 0.25
LOG2E = 1.0 / math.log(2.0)
AXES = ("loop", "slab")
X, Y, Z, C = 4, 4, 8, 2
TILE = 256
LANES = 128
MIB = 1 << 20


def place(device):
    loop, slab = divmod(device, Y * 2)
    z, rest = divmod(loop, 4)
    return (2 * (rest // 2) + slab % 2, slab // 2, z, rest % 2)


def device_at(x, y, z, core):
    return (z * 4 + (x // 2) * 2 + core) * (Y * 2) + y * 2 + x % 2


def send(block, target):
    route = [(d, device_at(*target(*place(d)))) for d in range(X * Y * Z * C)]
    return lax.ppermute(block, AXES, route)


def along_z(block, step):
    return send(block, lambda x, y, z, c: (x, y, (z + step) % Z, c))


def to_sibling(block):
    return send(block, lambda x, y, z, c: (x, y, z, 1 - c))


def groups_by(key):
    groups = {}
    for d in range(X * Y * Z * C):
        groups.setdefault(key(*place(d)), []).append(d)
    return list(groups.values())


def here(shape, dtype):
    return pltpu.VMEM(shape, dtype)


def pinned(*arrays):
    return [pltpu.with_memory_space_constraint(a, pltpu.VMEM) for a in arrays]


IN_VMEM = pl.BlockSpec(memory_space=pltpu.VMEM)


def combine(parts):
    top = jnp.max(parts, axis=0)
    return top + jnp.log(jnp.sum(jnp.exp2(parts - top), axis=0)) * LOG2E


def squares_of(block):
    wide = block.astype(jnp.float32)
    return jnp.sum(wide * wide, axis=1, keepdims=True) * (SHARP / block.shape[1] * LOG2E)


def bias_kernel(cent_ref, bias_ref):
    bias_ref[...] = jnp.broadcast_to(squares_of(cent_ref[...]), bias_ref.shape)


def bias_of(cents):
    return pl.pallas_call(
        bias_kernel,
        in_specs=[IN_VMEM],
        out_specs=IN_VMEM,
        out_shape=here((cents.shape[0], LANES), jnp.float32),
        compiler_params=pltpu.CompilerParams(vmem_limit_bytes=8 * MIB),
        cost_estimate=pl.CostEstimate(flops=1, bytes_accessed=1, transcendentals=0),
    )(*pinned(cents))


def begin_kernel(point_ref, cent_ref, point_out, cent_out, bias_ref):
    point_out[...] = point_ref[...]
    cents = cent_ref[...]
    cent_out[...] = cents
    bias_ref[...] = jnp.broadcast_to(squares_of(cents), bias_ref.shape)


def begin(points, cents):
    return pl.pallas_call(
        begin_kernel,
        in_specs=[IN_VMEM, IN_VMEM],
        out_specs=(IN_VMEM,) * 3,
        out_shape=(
            here(points.shape, points.dtype),
            here(cents.shape, cents.dtype),
            here((cents.shape[0], LANES), jnp.float32),
        ),
        compiler_params=pltpu.CompilerParams(vmem_limit_bytes=8 * MIB),
        cost_estimate=pl.CostEstimate(flops=1, bytes_accessed=1, transcendentals=0),
    )(points, cents)


def logits_kernel(count, first, aliased, *refs):
    blocks = refs[:count]
    cent_refs, bias_refs = refs[count : count + 2], refs[count + 2 : count + 4]
    logits_ref, group_ref, norm_ref, xsq_ref = refs[count + 4 + 3 * aliased :]
    rows, width = blocks[0].shape
    points = rows * count
    scale = SHARP / width * LOG2E
    columns = pl.ds(first, points)
    for at, ref in enumerate(blocks):
        block = ref[...]
        group_ref[pl.ds(first + at * rows, rows), :] = block
        xsq_ref[:, pl.ds(at * rows, rows)] = jnp.broadcast_to(squares_of(block), (rows, LANES)).T[:8]
    group = group_ref[columns, :]
    xsq = xsq_ref[:1, :]
    half = cent_refs[0].shape[0] // TILE
    tiles = 2 * half
    high = None
    for t in range(tiles):
        here_rows, within = pl.ds(t * TILE, TILE), pl.ds(t % half * TILE, TILE)
        dots = lax.dot_general(
            cent_refs[t // half][within, :], group, (((1,), (1,)), ((), ())), preferred_element_type=jnp.float32
        )
        bias = jnp.concatenate([bias_refs[t // half][within, :]] * (points // LANES), axis=1)
        logits = 2.0 * scale * dots - (bias + xsq)
        logits_ref[here_rows, columns] = logits
        top = jnp.max(logits, axis=0, keepdims=True)
        high = top if high is None else jnp.maximum(high, top)
    total = None
    for t in range(tiles):
        part = jnp.sum(jnp.exp2(logits_ref[pl.ds(t * TILE, TILE), columns] - high), axis=0, keepdims=True)
        total = part if total is None else total + part
    norm_ref[:, columns] = high + jnp.log(total) * LOG2E


def logits_of(blocks, first, points, cents, bias, before):
    rows, width = blocks[0].shape
    count = 2 * cents[0].shape[0]
    more = rows * len(blocks)
    operands = [*blocks, *cents, *bias, *before]
    return pl.pallas_call(
        functools.partial(logits_kernel, len(blocks), first, len(before) > 0),
        in_specs=[IN_VMEM] * len(operands),
        out_specs=(IN_VMEM,) * 3,
        out_shape=(
            here((count, points), jnp.float32),
            here((points, width), blocks[0].dtype),
            here((1, points), jnp.float32),
        ),
        input_output_aliases={len(blocks) + 4 + k: k for k in range(len(before))},
        scratch_shapes=[pltpu.VMEM((8, more), jnp.float32)],
        compiler_params=pltpu.CompilerParams(vmem_limit_bytes=8 * MIB),
        cost_estimate=pl.CostEstimate(flops=2 * count * more * width, bytes_accessed=1, transcendentals=0),
    )(*pinned(*operands))


def row_of(offset, other):
    loop = lax.axis_index("loop")
    z, x_hi = loop // 4, (loop // 2) % 2
    plane = lax.rem(z + (offset % Z), Z)
    return 2 * plane + (1 - x_hi if other else x_hi)


def arrange_kernel(order, norm_ref, out_ref):
    for k, (offset, other) in enumerate(order):
        out_ref[pl.ds(row_of(offset, other), 1), :] = norm_ref[:, pl.ds(k * LANES, LANES)]


def arrange(order, norms):
    return pl.pallas_call(
        functools.partial(arrange_kernel, order),
        in_specs=[IN_VMEM],
        out_specs=IN_VMEM,
        out_shape=here((len(order), LANES), jnp.float32),
        compiler_params=pltpu.CompilerParams(vmem_limit_bytes=8 * MIB),
    )(*pinned(norms))


def spread_kernel(order, parts_ref, norm_ref, rows_ref):
    rows_ref[...] = combine(parts_ref[...])
    for k, (offset, other) in enumerate(order):
        row = rows_ref[pl.ds(row_of(offset, other), 1), :]
        norm_ref[:, pl.ds(k * LANES, LANES)] = jnp.broadcast_to(row, (8, LANES))


def add_up(logits_ref, start, group_ref, norm_ref, cent_ref, out_ref):
    rows, width = out_ref.shape[0], group_ref.shape[1]
    points = group_ref.shape[0]
    total, mass = None, None
    deep = 512
    for at in range(0, points, deep):
        columns = pl.ds(at, deep)
        logits = logits_ref[pl.ds(start, rows), columns]
        resp = jnp.exp2(logits - norm_ref[:1, columns]).astype(jnp.bfloat16)
        part = jnp.dot(resp, group_ref[columns, :], preferred_element_type=jnp.float32)
        wide = resp.astype(jnp.float32)
        weight = sum(wide[:, k : k + LANES] for k in range(0, deep, LANES))
        total = part if total is None else total + part
        mass = weight if mass is None else mass + weight
    mass = jnp.sum(mass, axis=1, keepdims=True)
    if cent_ref is not None:
        total = total + PRIOR * cent_ref[...].astype(jnp.float32)
        mass = mass + PRIOR
    out_ref[:, pl.ds(0, width)] = total
    out_ref[:, pl.ds(width, LANES)] = jnp.broadcast_to(mass, (rows, LANES))


def first_sums_kernel(order, start, logits_ref, group_ref, parts_ref, out_ref, norm_ref, rows_ref):
    spread_kernel(order, parts_ref, norm_ref, rows_ref)
    add_up(logits_ref, start, group_ref, norm_ref, None, out_ref)


def more_sums_kernel(start, logits_ref, group_ref, norm_ref, out_ref):
    add_up(logits_ref, start, group_ref, norm_ref, None, out_ref)


def own_sums_kernel(start, logits_ref, group_ref, norm_ref, cent_ref, out_ref):
    add_up(logits_ref, start, group_ref, norm_ref, cent_ref, out_ref)


def sums_call(kernel, operands, rows, points, width, spread=None):
    out = here((rows, width + LANES), jnp.float32)
    return pl.pallas_call(
        kernel,
        in_specs=[IN_VMEM] * len(operands),
        out_specs=(IN_VMEM, IN_VMEM) if spread else IN_VMEM,
        out_shape=(out, here((8, points), jnp.float32)) if spread else out,
        scratch_shapes=[pltpu.VMEM((spread, LANES), jnp.float32)] if spread else [],
        compiler_params=pltpu.CompilerParams(vmem_limit_bytes=16 * MIB),
        cost_estimate=pl.CostEstimate(flops=1, bytes_accessed=1, transcendentals=0),
    )(*pinned(*operands))


def finish_kernel(own_ref, *refs):
    out_ref = refs[-1]
    rows, width = out_ref.shape
    first = 0
    for ref in refs[:-1]:
        last = first + ref.shape[0]
        for step in range(own_ref.shape[0] // rows):
            start, stop = max(first, step * rows), min(last, (step + 1) * rows)
            if start >= stop:
                continue

            @pl.when(pl.program_id(0) == step)
            def _():
                both = own_ref[pl.ds(start, stop - start), :] + ref[pl.ds(start - first, stop - start), :]
                weight = 1.0 / both[:, width:]
                out_ref[pl.ds(start - step * rows, stop - start), :] = both[:, :width] * jnp.concatenate(
                    [weight] * (width // LANES), axis=1
                )

        first = last


def finish(own, others):
    rows, wide = own.shape
    width = wide - LANES
    steps = 2
    return pl.pallas_call(
        finish_kernel,
        grid=(steps,),
        in_specs=[IN_VMEM] * (1 + len(others)),
        out_specs=pl.BlockSpec((rows // steps, width), lambda i: (i, 0)),
        out_shape=jax.ShapeDtypeStruct((rows, width), jnp.float32),
        compiler_params=pltpu.CompilerParams(vmem_limit_bytes=8 * MIB),
        cost_estimate=pl.CostEstimate(flops=3 * rows * width, bytes_accessed=4 * rows * width, transcendentals=0),
    )(*pinned(own, *others))


def after(arrays, *done):
    return lax.optimization_barrier((arrays, done))[0]


def shards(points, centroids):
    rows = points.shape[0]
    everything = rows * Z * 2

    across = send(points, lambda x, y, z, c: (3 - x, y, z, c))
    other_cents = to_sibling(centroids)
    held, own_cents, own_bias = begin(points, centroids)
    cents, bias = (other_cents, own_cents), (bias_of(other_cents), own_bias)

    order, state = [], []

    def take(blocks, places):
        nonlocal state
        first = rows * len(order)
        order.extend(places)
        state = logits_of(blocks, first, everything, cents, bias, state)

    own, far = [points, points], [across, across]
    both_ways = lambda pair: [along_z(pair[0], 1), along_z(pair[1], -1)]
    own = both_ways(own)
    far = both_ways(after(far, held))
    pending = [([held, across], [(0, 0), (0, 1)])]
    for step in (1, 2, 3):
        seen = [] if step == 1 else state[2]
        if step < 3:
            next_own = both_ways(after(own, seen))
        else:
            next_own = [along_z(own[0], 1)]
        take(*pending.pop(0))
        seen = state[2]
        if step < 3:
            next_far = both_ways(after(far, seen))
        else:
            next_far = [along_z(after(far[1], seen), -1)]
        if step > 1:
            take(*pending.pop(0))
        pending.append((own, [(-step, 0), (step, 0)]))
        pending.append((far, [(-step, 1), (step, 1)]))
        own, far = next_own, next_far
    pending.append(([own[0], far[0]], [(4, 0), (4, 1)]))
    for blocks, places in pending:
        take(blocks, places)
    logits, blocks, norms = state

    local = arrange(order, norms)
    local = combine(
        jnp.stack([local] + [send(local, lambda x, y, z, c, k=k: ((x + k) % X, y, z, c)) for k in (2, 1, 3)])
    )
    everywhere = jnp.broadcast_to(local[None], (Y * Z,) + local.shape)
    parts = lax.all_to_all(everywhere, AXES, 0, 0, axis_index_groups=groups_by(lambda x, y, z, c: (x, c)))

    count, width = centroids.shape
    piece = count * 5 // 8
    shape = (everything, width)
    one, norm = sums_call(
        functools.partial(first_sums_kernel, tuple(order), 0), (logits, blocks, parts), piece, *shape, len(order)
    )
    got_one = to_sibling(one)
    two = sums_call(functools.partial(more_sums_kernel, piece), (logits, blocks, norm), count - piece, *shape)
    got_two = to_sibling(two)
    norm = after(norm, two)
    own_sums = sums_call(
        functools.partial(own_sums_kernel, count), (logits, blocks, norm, own_cents), count, *shape
    )
    return finish(own_sums, (got_one, got_two))


def solution(mesh):
    return jax.shard_map(
        shards,
        mesh=mesh,
        in_specs=(P("loop", None), P(("loop", "slab"), None)),
        out_specs=P(("loop", "slab"), None),
        check_vma=False,
    )
```

```python
import functools
import math

import jax
import jax.numpy as jnp
from jax import lax
from jax.experimental import pallas as pl
from jax.experimental.pallas import tpu as pltpu
from jax.sharding import PartitionSpec as P

SHARP = 20.0
PRIOR = 0.25
LOG2E = 1.0 / math.log(2.0)
AXES = ("loop", "slab")
X, Y, Z, C = 4, 4, 8, 2
TILE = 256
LANES = 128
MIB = 1 << 20


def place(device):
    loop, slab = divmod(device, Y * 2)
    z, rest = divmod(loop, 4)
    return (2 * (rest // 2) + slab % 2, slab // 2, z, rest % 2)


def device_at(x, y, z, core):
    return (z * 4 + (x // 2) * 2 + core) * (Y * 2) + y * 2 + x % 2


def send(block, target):
    route = [(d, device_at(*target(*place(d)))) for d in range(X * Y * Z * C)]
    return lax.ppermute(block, AXES, route)


def along_z(block, step):
    return send(block, lambda x, y, z, c: (x, y, (z + step) % Z, c))


def to_sibling(block):
    return send(block, lambda x, y, z, c: (x, y, z, 1 - c))


def groups_by(key):
    groups = {}
    for d in range(X * Y * Z * C):
        groups.setdefault(key(*place(d)), []).append(d)
    return list(groups.values())


def here(shape, dtype):
    return pltpu.VMEM(shape, dtype)


def pinned(*arrays):
    return [pltpu.with_memory_space_constraint(a, pltpu.VMEM) for a in arrays]


IN_VMEM = pl.BlockSpec(memory_space=pltpu.VMEM)


def combine(parts):
    top = jnp.max(parts, axis=0)
    return top + jnp.log(jnp.sum(jnp.exp2(parts - top), axis=0)) * LOG2E


def squares_of(block):
    wide = block.astype(jnp.float32)
    return jnp.sum(wide * wide, axis=1, keepdims=True) * (SHARP / block.shape[1] * LOG2E)


def bias_kernel(cent_ref, bias_ref):
    bias_ref[...] = jnp.broadcast_to(squares_of(cent_ref[...]), bias_ref.shape)


def bias_of(cents):
    return pl.pallas_call(
        bias_kernel,
        in_specs=[IN_VMEM],
        out_specs=IN_VMEM,
        out_shape=here((cents.shape[0], LANES), jnp.float32),
        compiler_params=pltpu.CompilerParams(vmem_limit_bytes=8 * MIB),
        cost_estimate=pl.CostEstimate(flops=1, bytes_accessed=1, transcendentals=0),
    )(*pinned(cents))


def begin_kernel(point_ref, cent_ref, point_out, cent_out, bias_ref):
    point_out[...] = point_ref[...]
    cents = cent_ref[...]
    cent_out[...] = cents
    bias_ref[...] = jnp.broadcast_to(squares_of(cents), bias_ref.shape)


def begin(points, cents):
    return pl.pallas_call(
        begin_kernel,
        in_specs=[IN_VMEM, IN_VMEM],
        out_specs=(IN_VMEM,) * 3,
        out_shape=(
            here(points.shape, points.dtype),
            here(cents.shape, cents.dtype),
            here((cents.shape[0], LANES), jnp.float32),
        ),
        compiler_params=pltpu.CompilerParams(vmem_limit_bytes=8 * MIB),
        cost_estimate=pl.CostEstimate(flops=1, bytes_accessed=1, transcendentals=0),
    )(points, cents)


def logits_kernel(count, first, aliased, *refs):
    blocks = refs[:count]
    cent_refs, bias_refs = refs[count : count + 2], refs[count + 2 : count + 4]
    logits_ref, group_ref, norm_ref, xsq_ref = refs[count + 4 + 3 * aliased :]
    rows, width = blocks[0].shape
    points = rows * count
    scale = SHARP / width * LOG2E
    columns = pl.ds(first, points)
    for at, ref in enumerate(blocks):
        block = ref[...]
        group_ref[pl.ds(first + at * rows, rows), :] = block
        xsq_ref[:, pl.ds(at * rows, rows)] = jnp.broadcast_to(squares_of(block), (rows, LANES)).T[:8]
    group = group_ref[columns, :]
    xsq = xsq_ref[:1, :]
    half = cent_refs[0].shape[0] // TILE
    tiles = 2 * half
    high = None
    for t in range(tiles):
        here_rows, within = pl.ds(t * TILE, TILE), pl.ds(t % half * TILE, TILE)
        dots = lax.dot_general(
            cent_refs[t // half][within, :], group, (((1,), (1,)), ((), ())), preferred_element_type=jnp.float32
        )
        bias = jnp.concatenate([bias_refs[t // half][within, :]] * (points // LANES), axis=1)
        logits = 2.0 * scale * dots - (bias + xsq)
        logits_ref[here_rows, columns] = logits
        top = jnp.max(logits, axis=0, keepdims=True)
        high = top if high is None else jnp.maximum(high, top)
    total = None
    for t in range(tiles):
        part = jnp.sum(jnp.exp2(logits_ref[pl.ds(t * TILE, TILE), columns] - high), axis=0, keepdims=True)
        total = part if total is None else total + part
    norm_ref[:, columns] = high + jnp.log(total) * LOG2E


def logits_of(blocks, first, points, cents, bias, before):
    rows, width = blocks[0].shape
    count = 2 * cents[0].shape[0]
    more = rows * len(blocks)
    operands = [*blocks, *cents, *bias, *before]
    return pl.pallas_call(
        functools.partial(logits_kernel, len(blocks), first, len(before) > 0),
        in_specs=[IN_VMEM] * len(operands),
        out_specs=(IN_VMEM,) * 3,
        out_shape=(
            here((count, points), jnp.float32),
            here((points, width), blocks[0].dtype),
            here((1, points), jnp.float32),
        ),
        input_output_aliases={len(blocks) + 4 + k: k for k in range(len(before))},
        scratch_shapes=[pltpu.VMEM((8, more), jnp.float32)],
        compiler_params=pltpu.CompilerParams(vmem_limit_bytes=8 * MIB),
        cost_estimate=pl.CostEstimate(flops=2 * count * more * width, bytes_accessed=1, transcendentals=0),
    )(*pinned(*operands))


def row_of(offset, other):
    loop = lax.axis_index("loop")
    z, x_hi = loop // 4, (loop // 2) % 2
    plane = lax.rem(z + (offset % Z), Z)
    return 2 * plane + (1 - x_hi if other else x_hi)


def arrange_kernel(order, norm_ref, out_ref):
    for k, (offset, other) in enumerate(order):
        out_ref[pl.ds(row_of(offset, other), 1), :] = norm_ref[:, pl.ds(k * LANES, LANES)]


def arrange(order, norms):
    return pl.pallas_call(
        functools.partial(arrange_kernel, order),
        in_specs=[IN_VMEM],
        out_specs=IN_VMEM,
        out_shape=here((len(order), LANES), jnp.float32),
        compiler_params=pltpu.CompilerParams(vmem_limit_bytes=8 * MIB),
    )(*pinned(norms))


def spread_kernel(order, parts_ref, norm_ref, rows_ref):
    rows_ref[...] = combine(parts_ref[...])
    for k, (offset, other) in enumerate(order):
        row = rows_ref[pl.ds(row_of(offset, other), 1), :]
        norm_ref[:, pl.ds(k * LANES, LANES)] = jnp.broadcast_to(row, (8, LANES))


def add_up(logits_ref, start, group_ref, norm_ref, cent_ref, out_ref):
    rows, width = out_ref.shape[0], group_ref.shape[1]
    points = group_ref.shape[0]
    some = TILE if rows % TILE == 0 else rows
    deep = points if rows % TILE == 0 else 512
    for first in range(0, rows, some):
        within = pl.ds(first, some)
        total, mass = None, None
        for at in range(0, points, deep):
            columns = pl.ds(at, deep)
            logits = logits_ref[pl.ds(start + first, some), columns]
            resp = jnp.exp2(logits - norm_ref[:1, columns]).astype(jnp.bfloat16)
            part = jnp.dot(resp, group_ref[columns, :], preferred_element_type=jnp.float32)
            wide = resp.astype(jnp.float32)
            weight = sum(wide[:, k : k + LANES] for k in range(0, deep, LANES))
            total = part if total is None else total + part
            mass = weight if mass is None else mass + weight
        mass = jnp.sum(mass, axis=1, keepdims=True)
        if cent_ref is not None:
            total = total + PRIOR * cent_ref[within, :].astype(jnp.float32)
            mass = mass + PRIOR
        out_ref[within, pl.ds(0, width)] = total
        out_ref[within, pl.ds(width, LANES)] = jnp.broadcast_to(mass, (some, LANES))


def first_sums_kernel(order, start, logits_ref, group_ref, parts_ref, out_ref, norm_ref, rows_ref):
    spread_kernel(order, parts_ref, norm_ref, rows_ref)
    add_up(logits_ref, start, group_ref, norm_ref, None, out_ref)


def more_sums_kernel(start, logits_ref, group_ref, norm_ref, out_ref):
    add_up(logits_ref, start, group_ref, norm_ref, None, out_ref)


def own_sums_kernel(start, logits_ref, group_ref, norm_ref, cent_ref, out_ref):
    add_up(logits_ref, start, group_ref, norm_ref, cent_ref, out_ref)


def sums_call(kernel, operands, rows, points, width, spread=None):
    out = here((rows, width + LANES), jnp.float32)
    return pl.pallas_call(
        kernel,
        in_specs=[IN_VMEM] * len(operands),
        out_specs=(IN_VMEM, IN_VMEM) if spread else IN_VMEM,
        out_shape=(out, here((8, points), jnp.float32)) if spread else out,
        scratch_shapes=[pltpu.VMEM((spread, LANES), jnp.float32)] if spread else [],
        compiler_params=pltpu.CompilerParams(vmem_limit_bytes=16 * MIB),
        cost_estimate=pl.CostEstimate(flops=1, bytes_accessed=1, transcendentals=0),
    )(*pinned(*operands))


def finish_kernel(own_ref, *refs):
    out_ref = refs[-1]
    rows, width = out_ref.shape
    first = 0
    for ref in refs[:-1]:
        last = first + ref.shape[0]
        for step in range(own_ref.shape[0] // rows):
            start, stop = max(first, step * rows), min(last, (step + 1) * rows)
            if start >= stop:
                continue

            @pl.when(pl.program_id(0) == step)
            def _():
                both = own_ref[pl.ds(start, stop - start), :] + ref[pl.ds(start - first, stop - start), :]
                weight = 1.0 / both[:, width:]
                out_ref[pl.ds(start - step * rows, stop - start), :] = both[:, :width] * jnp.concatenate(
                    [weight] * (width // LANES), axis=1
                )

        first = last


def finish(own, others):
    rows, wide = own.shape
    width = wide - LANES
    steps = 2
    return pl.pallas_call(
        finish_kernel,
        grid=(steps,),
        in_specs=[IN_VMEM] * (1 + len(others)),
        out_specs=pl.BlockSpec((rows // steps, width), lambda i: (i, 0)),
        out_shape=jax.ShapeDtypeStruct((rows, width), jnp.float32),
        compiler_params=pltpu.CompilerParams(vmem_limit_bytes=8 * MIB),
        cost_estimate=pl.CostEstimate(flops=3 * rows * width, bytes_accessed=4 * rows * width, transcendentals=0),
    )(*pinned(own, *others))


def after(arrays, *done):
    return lax.optimization_barrier((arrays, done))[0]


def shards(points, centroids):
    rows = points.shape[0]
    everything = rows * Z * 2

    across = send(points, lambda x, y, z, c: (3 - x, y, z, c))
    other_cents = to_sibling(centroids)
    held, own_cents, own_bias = begin(points, centroids)
    cents, bias = (other_cents, own_cents), (bias_of(other_cents), own_bias)

    order, state = [], []

    def take(blocks, places):
        nonlocal state
        first = rows * len(order)
        order.extend(places)
        state = logits_of(blocks, first, everything, cents, bias, state)

    own, far = [points, points], [across, across]
    both_ways = lambda pair: [along_z(pair[0], 1), along_z(pair[1], -1)]
    own = both_ways(own)
    far = both_ways(after(far, held))
    pending = [([held, across], [(0, 0), (0, 1)])]
    for step in (1, 2, 3):
        seen = [] if step == 1 else state[2]
        if step < 3:
            next_own = both_ways(after(own, seen))
        else:
            next_own = [along_z(own[0], 1)]
        take(*pending.pop(0))
        seen = state[2]
        if step < 3:
            next_far = both_ways(after(far, seen))
        else:
            next_far = [along_z(after(far[1], seen), -1)]
        if step > 1:
            take(*pending.pop(0))
        pending.append((own, [(-step, 0), (step, 0)]))
        pending.append((far, [(-step, 1), (step, 1)]))
        own, far = next_own, next_far
    pending.append(([own[0], far[0]], [(4, 0), (4, 1)]))
    for blocks, places in pending:
        take(blocks, places)
    logits, blocks, norms = state

    local = arrange(order, norms)
    local = combine(
        jnp.stack([local] + [send(local, lambda x, y, z, c, k=k: ((x + k) % X, y, z, c)) for k in (2, 1, 3)])
    )
    everywhere = jnp.broadcast_to(local[None], (Y * Z,) + local.shape)
    parts = lax.all_to_all(everywhere, AXES, 0, 0, axis_index_groups=groups_by(lambda x, y, z, c: (x, c)))

    count, width = centroids.shape
    piece = count * 5 // 8
    shape = (everything, width)
    one, norm = sums_call(
        functools.partial(first_sums_kernel, tuple(order), 0), (logits, blocks, parts), piece, *shape, len(order)
    )
    got_one = to_sibling(one)
    two = sums_call(functools.partial(more_sums_kernel, piece), (logits, blocks, norm), count - piece, *shape)
    got_two = to_sibling(two)
    norm = after(norm, two)
    own_sums = sums_call(
        functools.partial(own_sums_kernel, count), (logits, blocks, norm, own_cents), count, *shape
    )
    return finish(own_sums, (got_one, got_two))


def solution(mesh):
    return jax.shard_map(
        shards,
        mesh=mesh,
        in_specs=(P("loop", None), P(("loop", "slab"), None)),
        out_specs=P(("loop", "slab"), None),
        check_vma=False,
    )
```

```python
import functools
import math

import jax
import jax.numpy as jnp
from jax import lax
from jax.experimental import pallas as pl
from jax.experimental.pallas import tpu as pltpu
from jax.sharding import PartitionSpec as P

SHARP = 20.0
PRIOR = 0.25
LOG2E = 1.0 / math.log(2.0)
AXES = ("loop", "slab")
X, Y, Z, C = 4, 4, 8, 2
TILE = 256
LANES = 128
MIB = 1 << 20


def place(device):
    loop, slab = divmod(device, Y * 2)
    z, rest = divmod(loop, 4)
    return (2 * (rest // 2) + slab % 2, slab // 2, z, rest % 2)


def device_at(x, y, z, core):
    return (z * 4 + (x // 2) * 2 + core) * (Y * 2) + y * 2 + x % 2


def send(block, target):
    route = [(d, device_at(*target(*place(d)))) for d in range(X * Y * Z * C)]
    return lax.ppermute(block, AXES, route)


def along_z(block, step):
    return send(block, lambda x, y, z, c: (x, y, (z + step) % Z, c))


def to_sibling(block):
    return send(block, lambda x, y, z, c: (x, y, z, 1 - c))


def groups_by(key):
    groups = {}
    for d in range(X * Y * Z * C):
        groups.setdefault(key(*place(d)), []).append(d)
    return list(groups.values())


def here(shape, dtype):
    return pltpu.VMEM(shape, dtype)


def pinned(*arrays):
    return [pltpu.with_memory_space_constraint(a, pltpu.VMEM) for a in arrays]


IN_VMEM = pl.BlockSpec(memory_space=pltpu.VMEM)


def combine(parts):
    top = jnp.max(parts, axis=0)
    return top + jnp.log(jnp.sum(jnp.exp2(parts - top), axis=0)) * LOG2E


def squares_of(block):
    wide = block.astype(jnp.float32)
    return jnp.sum(wide * wide, axis=1, keepdims=True) * (SHARP / block.shape[1] * LOG2E)


def bias_kernel(cent_ref, bias_ref):
    bias_ref[...] = jnp.broadcast_to(squares_of(cent_ref[...]), bias_ref.shape)


def bias_of(cents):
    return pl.pallas_call(
        bias_kernel,
        in_specs=[IN_VMEM],
        out_specs=IN_VMEM,
        out_shape=here((cents.shape[0], LANES), jnp.float32),
        compiler_params=pltpu.CompilerParams(vmem_limit_bytes=8 * MIB),
        cost_estimate=pl.CostEstimate(flops=1, bytes_accessed=1, transcendentals=0),
    )(*pinned(cents))


def begin_kernel(point_ref, cent_ref, point_out, cent_out, bias_ref):
    point_out[...] = point_ref[...]
    cents = cent_ref[...]
    cent_out[...] = cents
    bias_ref[...] = jnp.broadcast_to(squares_of(cents), bias_ref.shape)


def begin(points, cents):
    return pl.pallas_call(
        begin_kernel,
        in_specs=[IN_VMEM, IN_VMEM],
        out_specs=(IN_VMEM,) * 3,
        out_shape=(
            here(points.shape, points.dtype),
            here(cents.shape, cents.dtype),
            here((cents.shape[0], LANES), jnp.float32),
        ),
        compiler_params=pltpu.CompilerParams(vmem_limit_bytes=8 * MIB),
        cost_estimate=pl.CostEstimate(flops=1, bytes_accessed=1, transcendentals=0),
    )(points, cents)


def logits_kernel(count, first, aliased, *refs):
    blocks = refs[:count]
    cent_refs, bias_refs = refs[count : count + 2], refs[count + 2 : count + 4]
    logits_ref, group_ref, norm_ref, xsq_ref = refs[count + 4 + 3 * aliased :]
    rows, width = blocks[0].shape
    points = rows * count
    scale = SHARP / width * LOG2E
    columns = pl.ds(first, points)
    for at, ref in enumerate(blocks):
        block = ref[...]
        group_ref[pl.ds(first + at * rows, rows), :] = block
        xsq_ref[:, pl.ds(at * rows, rows)] = jnp.broadcast_to(squares_of(block), (rows, LANES)).T[:8]
    group = group_ref[columns, :]
    xsq = xsq_ref[:1, :]
    half = cent_refs[0].shape[0] // TILE
    tiles = 2 * half
    high = None
    for t in range(tiles):
        here_rows, within = pl.ds(t * TILE, TILE), pl.ds(t % half * TILE, TILE)
        dots = lax.dot_general(
            cent_refs[t // half][within, :], group, (((1,), (1,)), ((), ())), preferred_element_type=jnp.float32
        )
        bias = jnp.concatenate([bias_refs[t // half][within, :]] * (points // LANES), axis=1)
        logits = 2.0 * scale * dots - (bias + xsq)
        logits_ref[here_rows, columns] = logits
        top = jnp.max(logits, axis=0, keepdims=True)
        high = top if high is None else jnp.maximum(high, top)
    total = None
    for t in range(tiles):
        part = jnp.sum(jnp.exp2(logits_ref[pl.ds(t * TILE, TILE), columns] - high), axis=0, keepdims=True)
        total = part if total is None else total + part
    norm_ref[:, columns] = high + jnp.log(total) * LOG2E


def logits_of(blocks, first, points, cents, bias, before):
    rows, width = blocks[0].shape
    count = 2 * cents[0].shape[0]
    more = rows * len(blocks)
    operands = [*blocks, *cents, *bias, *before]
    return pl.pallas_call(
        functools.partial(logits_kernel, len(blocks), first, len(before) > 0),
        in_specs=[IN_VMEM] * len(operands),
        out_specs=(IN_VMEM,) * 3,
        out_shape=(
            here((count, points), jnp.float32),
            here((points, width), blocks[0].dtype),
            here((1, points), jnp.float32),
        ),
        input_output_aliases={len(blocks) + 4 + k: k for k in range(len(before))},
        scratch_shapes=[pltpu.VMEM((8, more), jnp.float32)],
        compiler_params=pltpu.CompilerParams(vmem_limit_bytes=8 * MIB),
        cost_estimate=pl.CostEstimate(flops=2 * count * more * width, bytes_accessed=1, transcendentals=0),
    )(*pinned(*operands))


def row_of(offset, other):
    loop = lax.axis_index("loop")
    z, x_hi = loop // 4, (loop // 2) % 2
    plane = lax.rem(z + (offset % Z), Z)
    return 2 * plane + (1 - x_hi if other else x_hi)


def arrange_kernel(order, norm_ref, out_ref):
    for k, (offset, other) in enumerate(order):
        out_ref[pl.ds(row_of(offset, other), 1), :] = norm_ref[:, pl.ds(k * LANES, LANES)]


def arrange(order, norms):
    return pl.pallas_call(
        functools.partial(arrange_kernel, order),
        in_specs=[IN_VMEM],
        out_specs=IN_VMEM,
        out_shape=here((len(order), LANES), jnp.float32),
        compiler_params=pltpu.CompilerParams(vmem_limit_bytes=8 * MIB),
    )(*pinned(norms))


def spread_kernel(order, parts_ref, norm_ref, rows_ref):
    rows_ref[...] = combine(parts_ref[...])
    for k, (offset, other) in enumerate(order):
        row = rows_ref[pl.ds(row_of(offset, other), 1), :]
        norm_ref[:, pl.ds(k * LANES, LANES)] = jnp.broadcast_to(row, (8, LANES))


def add_up(logits_ref, start, group_ref, norm_ref, cent_ref, out_ref):
    rows, width = out_ref.shape[0], group_ref.shape[1]
    points = group_ref.shape[0]
    some = TILE if rows % TILE == 0 else rows
    deep = points if rows % TILE == 0 else 512
    for first in range(0, rows, some):
        within = pl.ds(first, some)
        total, mass = None, None
        for at in range(0, points, deep):
            columns = pl.ds(at, deep)
            logits = logits_ref[pl.ds(start + first, some), columns]
            resp = jnp.exp2(logits - norm_ref[:1, columns]).astype(jnp.bfloat16)
            part = jnp.dot(resp, group_ref[columns, :], preferred_element_type=jnp.float32)
            wide = resp.astype(jnp.float32)
            weight = sum(wide[:, k : k + LANES] for k in range(0, deep, LANES))
            total = part if total is None else total + part
            mass = weight if mass is None else mass + weight
        mass = jnp.sum(mass, axis=1, keepdims=True)
        if cent_ref is not None:
            total = total + PRIOR * cent_ref[within, :].astype(jnp.float32)
            mass = mass + PRIOR
        out_ref[within, pl.ds(0, width)] = total
        out_ref[within, pl.ds(width, LANES)] = jnp.broadcast_to(mass, (some, LANES))


def first_sums_kernel(order, start, logits_ref, group_ref, parts_ref, out_ref, norm_ref, rows_ref):
    spread_kernel(order, parts_ref, norm_ref, rows_ref)
    add_up(logits_ref, start, group_ref, norm_ref, None, out_ref)


def more_sums_kernel(start, logits_ref, group_ref, norm_ref, out_ref):
    add_up(logits_ref, start, group_ref, norm_ref, None, out_ref)


def own_sums_kernel(start, logits_ref, group_ref, norm_ref, cent_ref, out_ref):
    add_up(logits_ref, start, group_ref, norm_ref, cent_ref, out_ref)


def sums_call(kernel, operands, rows, points, width, spread=None):
    out = here((rows, width + LANES), jnp.float32)
    return pl.pallas_call(
        kernel,
        in_specs=[IN_VMEM] * len(operands),
        out_specs=(IN_VMEM, IN_VMEM) if spread else IN_VMEM,
        out_shape=(out, here((8, points), jnp.float32)) if spread else out,
        scratch_shapes=[pltpu.VMEM((spread, LANES), jnp.float32)] if spread else [],
        compiler_params=pltpu.CompilerParams(vmem_limit_bytes=16 * MIB),
        cost_estimate=pl.CostEstimate(flops=1, bytes_accessed=1, transcendentals=0),
    )(*pinned(*operands))


def finish_kernel(own_ref, *refs):
    out_ref = refs[-1]
    rows, width = out_ref.shape
    first = 0
    for ref in refs[:-1]:
        last = first + ref.shape[0]
        for step in range(own_ref.shape[0] // rows):
            start, stop = max(first, step * rows), min(last, (step + 1) * rows)
            if start >= stop:
                continue

            @pl.when(pl.program_id(0) == step)
            def _():
                both = own_ref[pl.ds(start, stop - start), :] + ref[pl.ds(start - first, stop - start), :]
                weight = 1.0 / both[:, width:]
                out_ref[pl.ds(start - step * rows, stop - start), :] = both[:, :width] * jnp.concatenate(
                    [weight] * (width // LANES), axis=1
                )

        first = last


def finish(own, others):
    rows, wide = own.shape
    width = wide - LANES
    steps = 2
    return pl.pallas_call(
        finish_kernel,
        grid=(steps,),
        in_specs=[IN_VMEM] * (1 + len(others)),
        out_specs=pl.BlockSpec((rows // steps, width), lambda i: (i, 0)),
        out_shape=jax.ShapeDtypeStruct((rows, width), jnp.float32),
        compiler_params=pltpu.CompilerParams(vmem_limit_bytes=8 * MIB),
        cost_estimate=pl.CostEstimate(flops=3 * rows * width, bytes_accessed=4 * rows * width, transcendentals=0),
    )(*pinned(own, *others))


def after(arrays, *done):
    return lax.optimization_barrier((arrays, done))[0]


def shards(points, centroids):
    rows = points.shape[0]
    everything = rows * Z * 2

    across = send(points, lambda x, y, z, c: (3 - x, y, z, c))
    other_cents = to_sibling(centroids)
    held, own_cents, own_bias = begin(points, centroids)
    cents, bias = (other_cents, own_cents), (bias_of(other_cents), own_bias)

    order, state = [], []

    def take(blocks, places):
        nonlocal state
        first = rows * len(order)
        order.extend(places)
        state = logits_of(blocks, first, everything, cents, bias, state)

    own, far = [points, points], [across, across]
    both_ways = lambda pair: [along_z(pair[0], 1), along_z(pair[1], -1)]
    down_first = lambda pair: [along_z(pair[1], -1), along_z(pair[0], 1)][::-1]
    own = both_ways(own)
    far = down_first(after(far, held))
    pending = [([held, across], [(0, 0), (0, 1)])]
    for step in (1, 2, 3):
        seen = [] if step == 1 else state[2]
        if step < 3:
            next_own = both_ways(after(own, seen))
        else:
            next_own = [along_z(own[0], 1)]
        take(*pending.pop(0))
        seen = state[2]
        if step < 3:
            next_far = down_first(after(far, seen))
        else:
            next_far = [along_z(after(far[1], seen), -1)]
        if step > 1:
            take(*pending.pop(0))
        pending.append((own, [(-step, 0), (step, 0)]))
        pending.append((far, [(-step, 1), (step, 1)]))
        own, far = next_own, next_far
    pending.append(([own[0], far[0]], [(4, 0), (4, 1)]))
    for blocks, places in pending:
        take(blocks, places)
    logits, blocks, norms = state

    local = arrange(order, norms)
    local = combine(
        jnp.stack([local] + [send(local, lambda x, y, z, c, k=k: ((x + k) % X, y, z, c)) for k in (2, 1, 3)])
    )
    everywhere = jnp.broadcast_to(local[None], (Y * Z,) + local.shape)
    parts = lax.all_to_all(everywhere, AXES, 0, 0, axis_index_groups=groups_by(lambda x, y, z, c: (x, c)))

    count, width = centroids.shape
    piece = count * 5 // 8
    shape = (everything, width)
    one, norm = sums_call(
        functools.partial(first_sums_kernel, tuple(order), 0), (logits, blocks, parts), piece, *shape, len(order)
    )
    got_one = to_sibling(one)
    two = sums_call(functools.partial(more_sums_kernel, piece), (logits, blocks, norm), count - piece, *shape)
    got_two = to_sibling(two)
    norm = after(norm, two)
    own_sums = sums_call(
        functools.partial(own_sums_kernel, count), (logits, blocks, norm, own_cents), count, *shape
    )
    return finish(own_sums, (got_one, got_two))


def solution(mesh):
    return jax.shard_map(
        shards,
        mesh=mesh,
        in_specs=(P("loop", None), P(("loop", "slab"), None)),
        out_specs=P(("loop", "slab"), None),
        check_vma=False,
    )
```
